256 devices in a mesh: row: 32 (over x, y, core), col: 8 (over z).
Axes of the slice: x: 4, y: 4, z: 8, core: 2. Of those that a mesh axis runs over, the one named last changes fastest.
Arguments:
- activations: bfloat16 [512, 16384], P('row', 'col'), may hold values from -6 to 6
- output_gradient: bfloat16 [512, 16384], P('row', 'col'), may hold values from -6 to 6
- frozen_gate_weight: bfloat16 [16384, 26624], P('col', 'row'), may hold values from -0.046875 to 0.046875
- frozen_up_weight: bfloat16 [16384, 26624], P('col', 'row'), may hold values from -0.046875 to 0.046875
- frozen_down_weight: bfloat16 [26624, 16384], P('row', 'col'), may hold values from -0.0390625 to 0.0390625
- gate_adapter_first: bfloat16 [16384, 64], P('col'), may hold values from -0.046875 to 0.046875
- gate_adapter_second: bfloat16 [64, 26624], P(None, 'row'), may hold values from -0.75 to 0.75
- up_adapter_first: bfloat16 [16384, 64], P('col'), may hold values from -0.046875 to 0.046875
- up_adapter_second: bfloat16 [64, 26624], P(None, 'row'), may hold values from -0.75 to 0.75
- down_adapter_first: bfloat16 [26624, 64], P('row'), may hold values from -0.0390625 to 0.0390625
- down_leave: bfloat16 [64, 16384], P(None, 'col'), may hold values from -0.75 to 0.75
Outputs:
- activation_gradient: bfloat16 [512, 16384], P('row', 'col')
- gate_adapter_first_gradient: float32 [16384, 64], P(('col', 'row'))
- gate_adapter_second_gradient: float32 [64, 26624], P(None, 'row')
- up_adapter_first_gradient: float32 [16384, 64], P(('col', 'row'))
- up_adapter_second_gradient: float32 [64, 26624], P(None, 'row')
- down_adapter_first_gradient: float32 [26624, 64], P('row')
- down_adapter_second_gradient: float32 [64, 16384], P(None, ('col', 'row'))
The draws below stay inside these ranges and needn't reach their ends.
All inputs are finite; a program needn't handle non-finite values.
Results may differ from the reference program's by a relative error of at most 0.028.
Values may be sent and summed in bfloat16 or wider, within the bound.
No kernel may reach another device: no remote copies, remote signals or barrier semaphores. Data moves between devices by JAX's collectives and lax.ppermute only.
A program may use at most 128 MiB of HBM per device.

```python
import jax
import jax.numpy as jnp
from jax import lax

D = 16384
FF = 26624
R = 64
TOKENS = 512


def with_spikes(entries, rng, source, target, parts, factor):
    owner, partner = [(jnp.arange(entries.shape[position]) // (entries.shape[position] // parts)).reshape([-1 if axis == position else 1 for axis in range(entries.ndim)]) for position in (source, target)]
    chosen = jax.random.permutation(rng, parts)[partner]
    strong = (owner == chosen) | (owner == (partner + parts // 2) % parts)
    return jnp.where(strong, factor * entries, entries)


def levels(key, dims, shards, smallest, top_value):
    def one(axis_at, shards_of):
        steps = jax.random.uniform(jax.random.fold_in(jax.random.fold_in(key, 6), axis_at), (shards_of,), jnp.float32, smallest / len(shards), top_value / len(shards))
        return jnp.repeat(jnp.exp(steps), dims[axis_at] // shards_of).reshape((-1,) + (1,) * (len(dims) - axis_at - 1))

    loudness = one(*shards[0])
    for cut in shards[1:]:
        loudness = loudness * one(*cut)
    return loudness


def gaussian(stream_key, extent, width, limit, split=(), kind=jnp.bfloat16):
    result = width * jax.random.normal(stream_key, extent, jnp.float32)
    if split:
        result = result * levels(stream_key, extent, split, -0.22, 0.18)
    return jnp.clip(result, -limit, limit).astype(kind)


def gaussian_with(rng, shape, scale, most, split, heavy, kind=jnp.bfloat16):
    result = scale * jax.random.normal(rng, shape, jnp.float32)
    if split:
        result = result * levels(rng, shape, split, -0.22, 0.18)
    return jnp.clip(with_spikes(result, jax.random.fold_in(rng, 3), *heavy), -most, most).astype(kind)


def setup_inputs(seed: int = 0) -> dict:
    key_of = jax.random.split(jax.random.key(seed), 12)
    return {
        "activations": gaussian_with(key_of[0], (TOKENS, D), 1.0, 6.0, ((0, 32), (1, 8)), (1, 0, 32, 2.75)),
        "output_gradient": gaussian_with(key_of[1], (TOKENS, D), 1.0, 6.0, ((0, 32), (1, 8)), (1, 0, 32, 2.75)),
        "frozen_gate_weight": gaussian(key_of[2], (D, FF), D ** -0.5, 0.046875, ((0, 8), (1, 32))),
        "frozen_up_weight": gaussian(key_of[3], (D, FF), D ** -0.5, 0.046875, ((0, 8), (1, 32))),
        "frozen_down_weight": gaussian(key_of[4], (FF, D), FF ** -0.5, 0.0390625, ((0, 32), (1, 8))),
        "gate_adapter_first": gaussian(key_of[5], (D, R), D ** -0.5, 0.046875, ((0, 8),)),
        "gate_adapter_second": gaussian(key_of[6], (R, FF), R ** -0.5, 0.75, ((1, 32),)),
        "up_adapter_first": gaussian(key_of[7], (D, R), D ** -0.5, 0.046875, ((0, 8),)),
        "up_adapter_second": gaussian(key_of[8], (R, FF), R ** -0.5, 0.75, ((1, 32),)),
        "down_adapter_first": gaussian(key_of[9], (FF, R), FF ** -0.5, 0.0390625, ((0, 32),)),
        "down_leave": gaussian(key_of[10], (R, D), R ** -0.5, 0.75, ((1, 8),)),
    }


adapter_scale = 0.5


def matrix_multiply(left, right):
    return jnp.dot(left, right, preferred_element_type=jnp.float32)


def multiply_right_transposed(left, right):
    return lax.dot_general(left, right, (((1,), (1,)), ((), ())), preferred_element_type=jnp.float32)


def multiply_left_transposed(left, right):
    return lax.dot_general(left, right, (((0,), (0,)), ((), ())), preferred_element_type=jnp.float32)


def reference(activations, output_gradient, frozen_gate_weight, frozen_up_weight, frozen_down_weight, gate_adapter_first, gate_adapter_second, up_adapter_first, up_adapter_second, down_adapter_first, down_leave):
    gate_rank_product = matrix_multiply(activations, gate_adapter_first).astype(jnp.bfloat16)
    up_rank_product = matrix_multiply(activations, up_adapter_first).astype(jnp.bfloat16)
    down_rank_product = multiply_right_transposed(output_gradient, down_leave).astype(jnp.bfloat16)
    gate_activation = matrix_multiply(activations, frozen_gate_weight) + adapter_scale * matrix_multiply(gate_rank_product, gate_adapter_second)
    up_activation = matrix_multiply(activations, frozen_up_weight) + adapter_scale * matrix_multiply(up_rank_product, up_adapter_second)
    backward_result = multiply_right_transposed(output_gradient, frozen_down_weight) + adapter_scale * multiply_right_transposed(down_rank_product, down_adapter_first)
    sigmoid_gate = jax.nn.sigmoid(gate_activation)
    silu_gate = gate_activation * sigmoid_gate
    hidden_state = (silu_gate * up_activation).astype(jnp.bfloat16)
    up_gradient_term = (backward_result * silu_gate).astype(jnp.bfloat16)
    gate_gradient_term = (backward_result * up_activation * sigmoid_gate * (1.0 + gate_activation * (1.0 - sigmoid_gate))).astype(jnp.bfloat16)
    hidden_rank_product = matrix_multiply(hidden_state, down_adapter_first).astype(jnp.bfloat16)
    gate_backward = multiply_right_transposed(gate_gradient_term, gate_adapter_second).astype(jnp.bfloat16)
    up_backward = multiply_right_transposed(up_gradient_term, up_adapter_second).astype(jnp.bfloat16)
    activation_gradient = multiply_right_transposed(gate_gradient_term, frozen_gate_weight) + multiply_right_transposed(up_gradient_term, frozen_up_weight)
    activation_gradient = activation_gradient + adapter_scale * (multiply_right_transposed(gate_backward, gate_adapter_first) + multiply_right_transposed(up_backward, up_adapter_first))
    gate_adapter_first_gradient = adapter_scale * multiply_left_transposed(activations, gate_backward)
    up_adapter_first_gradient = adapter_scale * multiply_left_transposed(activations, up_backward)
    down_adapter_second_gradient = adapter_scale * multiply_left_transposed(hidden_rank_product, output_gradient)
    gate_adapter_second_gradient = adapter_scale * multiply_left_transposed(gate_rank_product, gate_gradient_term)
    up_adapter_second_gradient = adapter_scale * multiply_left_transposed(up_rank_product, up_gradient_term)
    down_adapter_first_gradient = adapter_scale * multiply_left_transposed(hidden_state, down_rank_product)
    return (activation_gradient.astype(jnp.bfloat16), gate_adapter_first_gradient, gate_adapter_second_gradient, up_adapter_first_gradient, up_adapter_second_gradient, down_adapter_first_gradient, down_adapter_second_gradient)
```

```python
import jax
import jax.numpy as jnp
from jax import lax
from jax.sharding import PartitionSpec as P

adapter_scale = 0.5


def matrix_multiply(left, right):
    return jnp.dot(left, right, preferred_element_type=jnp.float32)


def multiply_right_transposed(left, right):
    return lax.dot_general(
        left, right, (((1,), (1,)), ((), ())), preferred_element_type=jnp.float32
    )


def multiply_left_transposed(left, right):
    return lax.dot_general(
        left, right, (((0,), (0,)), ((), ())), preferred_element_type=jnp.float32
    )


def pointwise(gate_activation, up_activation, backward_result):
    sigmoid_gate = jax.nn.sigmoid(gate_activation)
    silu_gate = gate_activation * sigmoid_gate
    hidden_state = (silu_gate * up_activation).astype(jnp.bfloat16)
    up_gradient_term = (backward_result * silu_gate).astype(jnp.bfloat16)
    gate_gradient_term = (
        backward_result
        * up_activation
        * sigmoid_gate
        * (1.0 + gate_activation * (1.0 - sigmoid_gate))
    ).astype(jnp.bfloat16)
    return (hidden_state, gate_gradient_term, up_gradient_term)


def body(
    activations,
    output_gradient,
    frozen_gate_weight,
    frozen_up_weight,
    frozen_down_weight,
    gate_adapter_first,
    gate_adapter_second,
    up_adapter_first,
    up_adapter_second,
    down_adapter_first,
    down_leave,
):
    share_tokens, width = activations.shape
    rank, hidden_units = gate_adapter_second.shape
    row_count = lax.axis_size("row")
    tokens_all = share_tokens * row_count
    packed_width = hidden_units + rank

    both = lax.all_gather(
        jnp.concatenate([activations, output_gradient], axis=1), "row", axis=0, tiled=True
    )
    full_act = both[:, :width]
    full_out = both[:, width:]

    partial = jnp.concatenate(
        [
            matrix_multiply(full_act, frozen_gate_weight).astype(jnp.bfloat16),
            matrix_multiply(full_act, gate_adapter_first).astype(jnp.bfloat16),
            matrix_multiply(full_act, frozen_up_weight).astype(jnp.bfloat16),
            matrix_multiply(full_act, up_adapter_first).astype(jnp.bfloat16),
            multiply_right_transposed(full_out, frozen_down_weight).astype(jnp.bfloat16),
            multiply_right_transposed(full_out, down_leave).astype(jnp.bfloat16),
        ],
        axis=1,
    )
    totals = lax.psum_scatter(partial, "col", scatter_dimension=0, tiled=True)
    wide = [
        totals[:, i * packed_width : i * packed_width + hidden_units].astype(jnp.float32)
        for i in range(3)
    ]
    low = [totals[:, i * packed_width + hidden_units : (i + 1) * packed_width] for i in range(3)]
    gate_activation = wide[0] + adapter_scale * matrix_multiply(low[0], gate_adapter_second)
    up_activation = wide[1] + adapter_scale * matrix_multiply(low[1], up_adapter_second)
    backward_result = wide[2] + adapter_scale * multiply_right_transposed(
        low[2], down_adapter_first
    )
    hidden_state, gate_gradient_term, up_gradient_term = pointwise(
        gate_activation, up_activation, backward_result
    )
    packed = jnp.concatenate(
        [hidden_state, low[2], gate_gradient_term, low[0], up_gradient_term, low[1]], axis=1
    )
    piece = lax.all_gather(packed, "col", axis=0, tiled=True)
    piece_hidden, down_low, piece_gate, gate_low, piece_up, up_low = [
        piece[:, start : start + size]
        for i in range(3)
        for start, size in (
            (i * packed_width, hidden_units),
            (i * packed_width + hidden_units, rank),
        )
    ]

    share = jnp.concatenate(
        [
            (
                multiply_right_transposed(piece_gate, frozen_gate_weight)
                + multiply_right_transposed(piece_up, frozen_up_weight)
            ).astype(jnp.bfloat16),
            matrix_multiply(piece_hidden, down_adapter_first).astype(jnp.bfloat16),
            multiply_right_transposed(piece_gate, gate_adapter_second).astype(jnp.bfloat16),
            multiply_right_transposed(piece_up, up_adapter_second).astype(jnp.bfloat16),
        ],
        axis=1,
    )
    shares = lax.all_to_all(share, "row", 0, 0, tiled=True)
    summed = jnp.sum(
        shares.reshape(row_count, share_tokens, width + 3 * rank).astype(jnp.float32), axis=0
    )
    own_factors = summed[:, width:].astype(jnp.bfloat16)
    factors = lax.all_gather(own_factors, "row", axis=0, tiled=True)
    activation_gradient = (
        summed[:, :width]
        + adapter_scale
        * (
            multiply_right_transposed(own_factors[:, rank : 2 * rank], gate_adapter_first)
            + multiply_right_transposed(own_factors[:, 2 * rank :], up_adapter_first)
        )
    ).astype(jnp.bfloat16)

    gate_adapter_second_gradient = adapter_scale * multiply_left_transposed(gate_low, piece_gate)
    up_adapter_second_gradient = adapter_scale * multiply_left_transposed(up_low, piece_up)
    down_adapter_first_gradient = adapter_scale * multiply_left_transposed(piece_hidden, down_low)

    piece_width = width // row_count
    first_feature = lax.axis_index("row") * piece_width
    activation_columns = lax.dynamic_slice_in_dim(full_act, first_feature, piece_width, 1)
    output_columns = lax.dynamic_slice_in_dim(full_out, first_feature, piece_width, 1)
    gate_adapter_first_gradient = adapter_scale * multiply_left_transposed(
        activation_columns, factors[:, rank : 2 * rank]
    )
    up_adapter_first_gradient = adapter_scale * multiply_left_transposed(
        activation_columns, factors[:, 2 * rank :]
    )
    down_adapter_second_gradient = adapter_scale * multiply_left_transposed(
        factors[:, :rank], output_columns
    )
    return (
        activation_gradient,
        gate_adapter_first_gradient,
        gate_adapter_second_gradient,
        up_adapter_first_gradient,
        up_adapter_second_gradient,
        down_adapter_first_gradient,
        down_adapter_second_gradient,
    )


def solution(mesh):
    return jax.shard_map(
        body,
        mesh=mesh,
        in_specs=(
            P("row", "col"),
            P("row", "col"),
            P("col", "row"),
            P("col", "row"),
            P("row", "col"),
            P("col", None),
            P(None, "row"),
            P("col", None),
            P(None, "row"),
            P("row", None),
            P(None, "col"),
        ),
        out_specs=(
            P("row", "col"),
            P(("col", "row"), None),
            P(None, "row"),
            P(("col", "row"), None),
            P(None, "row"),
            P("row", None),
            P(None, ("col", "row")),
        ),
        check_vma=False,
    )
```

```python
import jax
import jax.numpy as jnp
from jax import lax
from jax.sharding import PartitionSpec as P

adapter_scale = 0.5


def matrix_multiply(left, right):
    return jnp.dot(left, right, preferred_element_type=jnp.float32)


def multiply_right_transposed(left, right):
    return lax.dot_general(
        left, right, (((1,), (1,)), ((), ())), preferred_element_type=jnp.float32
    )


def multiply_left_transposed(left, right):
    return lax.dot_general(
        left, right, (((0,), (0,)), ((), ())), preferred_element_type=jnp.float32
    )


def pointwise(gate_activation, up_activation, backward_result):
    sigmoid_gate = jax.nn.sigmoid(gate_activation)
    silu_gate = gate_activation * sigmoid_gate
    hidden_state = (silu_gate * up_activation).astype(jnp.bfloat16)
    up_gradient_term = (backward_result * silu_gate).astype(jnp.bfloat16)
    gate_gradient_term = (
        backward_result
        * up_activation
        * sigmoid_gate
        * (1.0 + gate_activation * (1.0 - sigmoid_gate))
    ).astype(jnp.bfloat16)
    return (hidden_state, gate_gradient_term, up_gradient_term)


def shifted(size, step):
    return [(i, (i + step) % size) for i in range(size)]


def ring_sum(partial, axis, share):
    size = lax.axis_size(axis)
    here = lax.axis_index(axis)

    def block(offset):
        start = lax.rem(here + offset + size, size) * share
        return lax.dynamic_slice_in_dim(partial, start, share, 0)

    up_steps = size // 2
    down_steps = size - 1 - up_steps
    up = block(up_steps).astype(jnp.bfloat16)
    down = block(-down_steps).astype(jnp.bfloat16)
    for step in range(1, up_steps + 1):
        up = lax.ppermute(up, axis, shifted(size, 1))
        if step <= down_steps:
            down = lax.ppermute(down, axis, shifted(size, -1))
        if step < up_steps:
            up = (up.astype(jnp.float32) + block(up_steps - step)).astype(jnp.bfloat16)
        if step < down_steps:
            down = (down.astype(jnp.float32) + block(step - down_steps)).astype(jnp.bfloat16)
    return up.astype(jnp.float32) + down.astype(jnp.float32) + block(0)


def body(
    activations,
    output_gradient,
    frozen_gate_weight,
    frozen_up_weight,
    frozen_down_weight,
    gate_adapter_first,
    gate_adapter_second,
    up_adapter_first,
    up_adapter_second,
    down_adapter_first,
    down_leave,
):
    share_tokens, width = activations.shape
    rank, hidden_units = gate_adapter_second.shape
    row_count = lax.axis_size("row")
    col_count = lax.axis_size("col")
    tokens_all = share_tokens * row_count
    col_tokens = tokens_all // col_count
    chips = row_count // 2
    core = lax.rem(lax.axis_index("row"), 2)

    both = lax.all_gather(
        jnp.concatenate([activations, output_gradient], axis=1), "row", axis=0, tiled=True
    )
    full_act = both[:, :width]
    full_out = both[:, width:]

    wide = []
    low = []
    for left, right in (
        (full_act, jnp.concatenate([frozen_gate_weight, gate_adapter_first], axis=1).T),
        (full_act, jnp.concatenate([frozen_up_weight, up_adapter_first], axis=1).T),
        (full_out, jnp.concatenate([frozen_down_weight, down_leave], axis=0)),
    ):
        total = ring_sum(multiply_right_transposed(left, right), "col", col_tokens)
        wide.append(total[:, :hidden_units])
        low.append(total[:, hidden_units:].astype(jnp.bfloat16))
    gate_activation = wide[0] + adapter_scale * matrix_multiply(low[0], gate_adapter_second)
    up_activation = wide[1] + adapter_scale * matrix_multiply(low[1], up_adapter_second)
    backward_result = wide[2] + adapter_scale * multiply_right_transposed(
        low[2], down_adapter_first
    )
    hidden_state, gate_gradient_term, up_gradient_term = pointwise(
        gate_activation, up_activation, backward_result
    )
    packed = jnp.concatenate(
        [gate_gradient_term, up_gradient_term, hidden_state, low[0], low[1], low[2]], axis=1
    )
    piece = lax.all_gather(packed, "col", axis=0, tiled=True)

    own_factors = jnp.concatenate(
        [
            matrix_multiply(hidden_state, down_adapter_first).astype(jnp.bfloat16),
            multiply_right_transposed(gate_gradient_term, gate_adapter_second).astype(jnp.bfloat16),
            multiply_right_transposed(up_gradient_term, up_adapter_second).astype(jnp.bfloat16),
        ],
        axis=1,
    )
    factor_parts = lax.all_to_all(
        jnp.broadcast_to(own_factors[None], (row_count,) + own_factors.shape),
        "row",
        0,
        0,
        tiled=True,
    )
    summed_factors = jnp.sum(factor_parts.astype(jnp.float32), axis=0).astype(jnp.bfloat16)
    factors = lax.all_to_all(
        jnp.broadcast_to(summed_factors[None], (col_count,) + summed_factors.shape),
        "col",
        0,
        0,
        tiled=True,
    ).reshape(tokens_all, 3 * rank)

    input_weight = jnp.concatenate([frozen_gate_weight, frozen_up_weight], axis=1)
    deltas = piece[:, : 2 * hidden_units].reshape(chips, 2, share_tokens, 2 * hidden_units)

    def tokens_of(which):
        chosen = lax.dynamic_slice_in_dim(deltas, which, 1, 1)
        return chosen.reshape(chips * share_tokens, 2 * hidden_units)

    other = multiply_right_transposed(tokens_of(1 - core), input_weight).astype(jnp.bfloat16)
    other = lax.ppermute(other, "row", [(i, i ^ 1) for i in range(row_count)])
    own = multiply_right_transposed(tokens_of(core), input_weight)
    share = (own + other.astype(jnp.float32)).astype(jnp.bfloat16)
    shares = lax.all_to_all(
        share,
        "row",
        0,
        0,
        axis_index_groups=[[2 * chip + c for chip in range(chips)] for c in range(2)],
        tiled=True,
    )
    summed = jnp.sum(
        shares.reshape(chips, share_tokens, width).astype(jnp.float32), axis=0
    )
    first_token = lax.axis_index("row") * share_tokens
    row_factors = lax.dynamic_slice_in_dim(factors, first_token, share_tokens, 0)
    activation_gradient = (
        summed
        + adapter_scale
        * (
            multiply_right_transposed(row_factors[:, rank : 2 * rank], gate_adapter_first)
            + multiply_right_transposed(row_factors[:, 2 * rank :], up_adapter_first)
        )
    ).astype(jnp.bfloat16)

    piece_gate = piece[:, :hidden_units]
    piece_up = piece[:, hidden_units : 2 * hidden_units]
    piece_hidden = piece[:, 2 * hidden_units : 3 * hidden_units]
    gate_low = piece[:, 3 * hidden_units : 3 * hidden_units + rank]
    up_low = piece[:, 3 * hidden_units + rank : 3 * hidden_units + 2 * rank]
    down_low = piece[:, 3 * hidden_units + 2 * rank :]
    gate_adapter_second_gradient = adapter_scale * multiply_left_transposed(gate_low, piece_gate)
    up_adapter_second_gradient = adapter_scale * multiply_left_transposed(up_low, piece_up)
    down_adapter_first_gradient = adapter_scale * multiply_left_transposed(piece_hidden, down_low)

    piece_width = width // row_count
    first_feature = lax.axis_index("row") * piece_width
    activation_columns = lax.dynamic_slice_in_dim(full_act, first_feature, piece_width, 1)
    output_columns = lax.dynamic_slice_in_dim(full_out, first_feature, piece_width, 1)
    gate_adapter_first_gradient = adapter_scale * multiply_left_transposed(
        activation_columns, factors[:, rank : 2 * rank]
    )
    up_adapter_first_gradient = adapter_scale * multiply_left_transposed(
        activation_columns, factors[:, 2 * rank :]
    )
    down_adapter_second_gradient = adapter_scale * multiply_left_transposed(
        factors[:, :rank], output_columns
    )
    return (
        activation_gradient,
        gate_adapter_first_gradient,
        gate_adapter_second_gradient,
        up_adapter_first_gradient,
        up_adapter_second_gradient,
        down_adapter_first_gradient,
        down_adapter_second_gradient,
    )


def solution(mesh):
    return jax.shard_map(
        body,
        mesh=mesh,
        in_specs=(
            P("row", "col"),
            P("row", "col"),
            P("col", "row"),
            P("col", "row"),
            P("row", "col"),
            P("col", None),
            P(None, "row"),
            P("col", None),
            P(None, "row"),
            P("row", None),
            P(None, "col"),
        ),
        out_specs=(
            P("row", "col"),
            P(("col", "row"), None),
            P(None, "row"),
            P(("col", "row"), None),
            P(None, "row"),
            P("row", None),
            P(None, ("col", "row")),
        ),
        check_vma=False,
    )
```

```python
import math

import jax
import jax.numpy as jnp
from jax import lax
from jax.sharding import PartitionSpec as P

adapter_scale = 0.5


def matrix_multiply(left, right):
    return jnp.dot(left, right, preferred_element_type=jnp.float32)


def multiply_right_transposed(left, right):
    return lax.dot_general(
        left, right, (((1,), (1,)), ((), ())), preferred_element_type=jnp.float32
    )


def multiply_left_transposed(left, right):
    return lax.dot_general(
        left, right, (((0,), (0,)), ((), ())), preferred_element_type=jnp.float32
    )


def pointwise(gate_activation, up_activation, backward_result):
    sigmoid_gate = jax.nn.sigmoid(gate_activation)
    silu_gate = gate_activation * sigmoid_gate
    hidden_state = (silu_gate * up_activation).astype(jnp.bfloat16)
    up_gradient_term = (backward_result * silu_gate).astype(jnp.bfloat16)
    gate_gradient_term = (
        backward_result
        * up_activation
        * sigmoid_gate
        * (1.0 + gate_activation * (1.0 - sigmoid_gate))
    ).astype(jnp.bfloat16)
    return (hidden_state, gate_gradient_term, up_gradient_term)


def shifted(size, step):
    return [(i, (i + step) % size) for i in range(size)]


def ring_sum(block_of, axis):
    size = lax.axis_size(axis)
    here = lax.axis_index(axis)

    def block(offset):
        return block_of(lax.rem(here + offset + size, size))

    up_steps = size // 2
    down_steps = size - 1 - up_steps
    up = block(up_steps).astype(jnp.bfloat16)
    down = block(-down_steps).astype(jnp.bfloat16)
    for step in range(1, up_steps + 1):
        up = lax.ppermute(up, axis, shifted(size, 1))
        if step <= down_steps:
            down = lax.ppermute(down, axis, shifted(size, -1))
        if step < up_steps:
            up = (up.astype(jnp.float32) + block(up_steps - step)).astype(jnp.bfloat16)
        if step < down_steps:
            down = (down.astype(jnp.float32) + block(step - down_steps)).astype(jnp.bfloat16)
    return up.astype(jnp.float32) + down.astype(jnp.float32) + block(0)


def gather_tokens(activations, output_gradient):
    tokens, width = activations.shape
    row_count = lax.axis_size("row")
    side = math.isqrt(row_count // 2)
    here = lax.axis_index("row")
    core = lax.rem(here, 2)
    x = here // (2 * side)
    y = lax.rem(here // 2, side)
    first_at = jnp.where(core == 0, x, y)
    second_at = jnp.where(core == 0, y, x)

    def moves(first, second):
        pairs = []
        for source in range(row_count):
            sx, sy, sc = source // (2 * side), source // 2 % side, source % 2
            step_x, step_y = (first, second) if sc == 0 else (second, first)
            pairs.append(
                (source, (((sx + step_x) % side) * side + (sy + step_y) % side) * 2 + sc)
            )
        return pairs

    swap = [(source, source ^ 1) for source in range(row_count)]

    def to_other_core(value):
        return lax.ppermute(value, "row", swap)

    mine = jnp.where(core == 0, activations, output_gradient)
    given = to_other_core(jnp.where(core == 0, output_gradient, activations))
    pair = jnp.concatenate(
        [jnp.where(core == 0, mine, given), jnp.where(core == 0, given, mine)], axis=0
    )
    slab = jnp.zeros((side,) + pair.shape, pair.dtype)
    slab = lax.dynamic_update_index_in_dim(slab, pair, first_at, 0)
    for step in (1, -1, 2):
        got = lax.ppermute(pair, "row", moves(step, 0))
        slab = lax.dynamic_update_index_in_dim(
            slab, got, lax.rem(first_at - step + side, side), 0
        )
    slab = slab.reshape(side * 2 * tokens, width)
    half = slab.shape[0] // 2

    before = lax.ppermute(slab, "row", moves(0, 1))
    after = lax.ppermute(slab, "row", moves(0, -1))
    far = jnp.concatenate(
        [
            lax.ppermute(before[:half], "row", moves(0, 1)),
            lax.ppermute(after[half:], "row", moves(0, -1)),
        ],
        axis=0,
    )
    gathered = jnp.zeros((2, side) + slab.shape, slab.dtype)
    for offset, part in ((0, slab), (-1, before), (1, after), (2, far)):
        for which, value, at in (
            (core, part, second_at),
            (1 - core, to_other_core(part), first_at),
        ):
            gathered = lax.dynamic_update_slice(
                gathered, value[None, None], (which, lax.rem(at + offset + side, side), 0, 0)
            )
    shape = (side, side, 2 * tokens, width)
    return gathered[0].reshape(shape), gathered[1].reshape(shape)


def body(
    activations,
    output_gradient,
    frozen_gate_weight,
    frozen_up_weight,
    frozen_down_weight,
    gate_adapter_first,
    gate_adapter_second,
    up_adapter_first,
    up_adapter_second,
    down_adapter_first,
    down_leave,
):
    share_tokens, width = activations.shape
    rank, hidden_units = gate_adapter_second.shape
    row_count = lax.axis_size("row")
    col_count = lax.axis_size("col")
    tokens_all = share_tokens * row_count
    col_tokens = tokens_all // col_count
    chips = row_count // 2
    core = lax.rem(lax.axis_index("row"), 2)

    gathered_act, gathered_out = gather_tokens(activations, output_gradient)
    side = gathered_act.shape[0]
    pair_tokens = 2 * share_tokens
    pairs_per_col = col_tokens // pair_tokens
    blocks_per_line = side // pairs_per_col
    full_act = gathered_act.reshape(tokens_all, width)
    full_out = gathered_out.reshape(tokens_all, width)

    def block_of_act(partial):
        lines = partial.reshape(side, side, pair_tokens, -1)

        def block_of(index):
            place = (lax.rem(index, blocks_per_line) * pairs_per_col, index // blocks_per_line)
            chosen = lax.dynamic_slice(
                lines, place + (0, 0), (pairs_per_col, 1, pair_tokens, lines.shape[3])
            )
            return chosen.reshape(col_tokens, -1)

        return block_of

    def block_of_out(partial):
        return lambda index: lax.dynamic_slice_in_dim(partial, index * col_tokens, col_tokens, 0)

    wide = []
    low = []
    for blocks, left, right in (
        (block_of_act, full_act, jnp.concatenate([frozen_gate_weight, gate_adapter_first], axis=1).T),
        (block_of_act, full_act, jnp.concatenate([frozen_up_weight, up_adapter_first], axis=1).T),
        (block_of_out, full_out, jnp.concatenate([frozen_down_weight, down_leave], axis=0)),
    ):
        partial = lax.optimization_barrier(multiply_right_transposed(left, right))
        total = ring_sum(blocks(partial), "col")
        wide.append(total[:, :hidden_units])
        low.append(total[:, hidden_units:].astype(jnp.bfloat16))
    gate_activation = wide[0] + adapter_scale * matrix_multiply(low[0], gate_adapter_second)
    up_activation = wide[1] + adapter_scale * matrix_multiply(low[1], up_adapter_second)
    backward_result = wide[2] + adapter_scale * multiply_right_transposed(
        low[2], down_adapter_first
    )
    hidden_state, gate_gradient_term, up_gradient_term = pointwise(
        gate_activation, up_activation, backward_result
    )
    packed = jnp.concatenate(
        [gate_gradient_term, up_gradient_term, hidden_state, low[0], low[1], low[2]], axis=1
    )
    piece = lax.all_gather(packed, "col", axis=0, tiled=True)

    own_factors = jnp.concatenate(
        [
            matrix_multiply(hidden_state, down_adapter_first).astype(jnp.bfloat16),
            multiply_right_transposed(gate_gradient_term, gate_adapter_second).astype(jnp.bfloat16),
            multiply_right_transposed(up_gradient_term, up_adapter_second).astype(jnp.bfloat16),
        ],
        axis=1,
    )
    factor_parts = lax.all_to_all(
        jnp.broadcast_to(own_factors[None], (row_count,) + own_factors.shape),
        "row",
        0,
        0,
        tiled=True,
    )
    summed_factors = jnp.sum(factor_parts.astype(jnp.float32), axis=0).astype(jnp.bfloat16)
    factors = lax.all_to_all(
        jnp.broadcast_to(summed_factors[None], (col_count,) + summed_factors.shape),
        "col",
        0,
        0,
        tiled=True,
    ).reshape(tokens_all, 3 * rank)

    input_weight = jnp.concatenate([frozen_gate_weight, frozen_up_weight], axis=1)
    deltas = piece[:, : 2 * hidden_units].reshape(chips, 2, share_tokens, 2 * hidden_units)

    def tokens_of(which):
        chosen = lax.dynamic_slice_in_dim(deltas, which, 1, 1)
        return chosen.reshape(chips * share_tokens, 2 * hidden_units)

    other = multiply_right_transposed(tokens_of(1 - core), input_weight).astype(jnp.bfloat16)
    other = lax.ppermute(other, "row", [(i, i ^ 1) for i in range(row_count)])
    own = multiply_right_transposed(tokens_of(core), input_weight)
    share = (own + other.astype(jnp.float32)).astype(jnp.bfloat16)
    shares = lax.all_to_all(
        share,
        "row",
        0,
        0,
        axis_index_groups=[[2 * chip + c for chip in range(chips)] for c in range(2)],
        tiled=True,
    )
    summed = jnp.sum(
        shares.reshape(chips, share_tokens, width).astype(jnp.float32), axis=0
    )
    first_token = lax.axis_index("row") * share_tokens
    row_factors = lax.dynamic_slice_in_dim(factors, first_token, share_tokens, 0)
    activation_gradient = (
        summed
        + adapter_scale
        * (
            multiply_right_transposed(row_factors[:, rank : 2 * rank], gate_adapter_first)
            + multiply_right_transposed(row_factors[:, 2 * rank :], up_adapter_first)
        )
    ).astype(jnp.bfloat16)

    piece_gate = piece[:, :hidden_units]
    piece_up = piece[:, hidden_units : 2 * hidden_units]
    piece_hidden = piece[:, 2 * hidden_units : 3 * hidden_units]
    gate_low = piece[:, 3 * hidden_units : 3 * hidden_units + rank]
    up_low = piece[:, 3 * hidden_units + rank : 3 * hidden_units + 2 * rank]
    down_low = piece[:, 3 * hidden_units + 2 * rank :]
    gate_adapter_second_gradient = adapter_scale * multiply_left_transposed(gate_low, piece_gate)
    up_adapter_second_gradient = adapter_scale * multiply_left_transposed(up_low, piece_up)
    down_adapter_first_gradient = adapter_scale * multiply_left_transposed(piece_hidden, down_low)

    piece_width = width // row_count
    first_feature = lax.axis_index("row") * piece_width
    activation_columns = lax.dynamic_slice_in_dim(full_act, first_feature, piece_width, 1)
    activation_columns = activation_columns.reshape(side, side, pair_tokens, piece_width)
    activation_columns = activation_columns.swapaxes(0, 1).reshape(tokens_all, piece_width)
    output_columns = lax.dynamic_slice_in_dim(full_out, first_feature, piece_width, 1)
    gate_adapter_first_gradient = adapter_scale * multiply_left_transposed(
        activation_columns, factors[:, rank : 2 * rank]
    )
    up_adapter_first_gradient = adapter_scale * multiply_left_transposed(
        activation_columns, factors[:, 2 * rank :]
    )
    down_adapter_second_gradient = adapter_scale * multiply_left_transposed(
        factors[:, :rank], output_columns
    )
    return (
        activation_gradient,
        gate_adapter_first_gradient,
        gate_adapter_second_gradient,
        up_adapter_first_gradient,
        up_adapter_second_gradient,
        down_adapter_first_gradient,
        down_adapter_second_gradient,
    )


def solution(mesh):
    return jax.shard_map(
        body,
        mesh=mesh,
        in_specs=(
            P("row", "col"),
            P("row", "col"),
            P("col", "row"),
            P("col", "row"),
            P("row", "col"),
            P("col", None),
            P(None, "row"),
            P("col", None),
            P(None, "row"),
            P("row", None),
            P(None, "col"),
        ),
        out_specs=(
            P("row", "col"),
            P(("col", "row"), None),
            P(None, "row"),
            P(("col", "row"), None),
            P(None, "row"),
            P("row", None),
            P(None, ("col", "row")),
        ),
        check_vma=False,
    )
```

```python
import math

import jax
import jax.numpy as jnp
from jax import lax
from jax.sharding import PartitionSpec as P

adapter_scale = 0.5


def matrix_multiply(left, right):
    return jnp.dot(left, right, preferred_element_type=jnp.float32)


def multiply_right_transposed(left, right):
    return lax.dot_general(
        left, right, (((1,), (1,)), ((), ())), preferred_element_type=jnp.float32
    )


def multiply_left_transposed(left, right):
    return lax.dot_general(
        left, right, (((0,), (0,)), ((), ())), preferred_element_type=jnp.float32
    )


def pointwise(gate_activation, up_activation, backward_result):
    sigmoid_gate = jax.nn.sigmoid(gate_activation)
    silu_gate = gate_activation * sigmoid_gate
    hidden_state = (silu_gate * up_activation).astype(jnp.bfloat16)
    up_gradient_term = (backward_result * silu_gate).astype(jnp.bfloat16)
    gate_gradient_term = (
        backward_result
        * up_activation
        * sigmoid_gate
        * (1.0 + gate_activation * (1.0 - sigmoid_gate))
    ).astype(jnp.bfloat16)
    return (hidden_state, gate_gradient_term, up_gradient_term)


def shifted(size, step):
    return [(i, (i + step) % size) for i in range(size)]


def ring_sum(block_of, axis, up_steps):
    size = lax.axis_size(axis)
    here = lax.axis_index(axis)
    down_steps = size - 1 - up_steps

    def block(offset):
        return block_of(lax.rem(here + offset + size, size))

    up = block(up_steps).astype(jnp.bfloat16)
    down = block(-down_steps).astype(jnp.bfloat16)
    for step in range(1, max(up_steps, down_steps) + 1):
        if step <= up_steps:
            up = lax.ppermute(up, axis, shifted(size, 1))
        if step <= down_steps:
            down = lax.ppermute(down, axis, shifted(size, -1))
        if step < up_steps:
            up = (up.astype(jnp.float32) + block(up_steps - step)).astype(jnp.bfloat16)
        if step < down_steps:
            down = (down.astype(jnp.float32) + block(step - down_steps)).astype(jnp.bfloat16)
    return up.astype(jnp.float32) + down.astype(jnp.float32) + block(0)


def ring_gather(block, axis, up_steps):
    size = lax.axis_size(axis)
    here = lax.axis_index(axis)
    down_steps = size - 1 - up_steps
    gathered = jnp.zeros((size,) + block.shape, block.dtype)
    gathered = lax.dynamic_update_index_in_dim(gathered, block, here, 0)
    up = down = block
    for step in range(1, max(up_steps, down_steps) + 1):
        if step <= up_steps:
            up = lax.ppermute(up, axis, shifted(size, 1))
        if step <= down_steps:
            down = lax.ppermute(down, axis, shifted(size, -1))
        if step <= up_steps:
            gathered = lax.dynamic_update_index_in_dim(
                gathered, up, lax.rem(here - step + size, size), 0
            )
        if step <= down_steps:
            gathered = lax.dynamic_update_index_in_dim(
                gathered, down, lax.rem(here + step, size), 0
            )
    return gathered.reshape((size * block.shape[0],) + block.shape[1:])


def gather_tokens(activations, output_gradient):
    tokens, width = activations.shape
    row_count = lax.axis_size("row")
    side = math.isqrt(row_count // 2)
    here = lax.axis_index("row")
    core = lax.rem(here, 2)
    x = here // (2 * side)
    y = lax.rem(here // 2, side)
    first_at = jnp.where(core == 0, x, y)
    second_at = jnp.where(core == 0, y, x)

    def moves(first, second):
        pairs = []
        for source in range(row_count):
            sx, sy, sc = source // (2 * side), source // 2 % side, source % 2
            step_x, step_y = (first, second) if sc == 0 else (second, first)
            pairs.append(
                (source, (((sx + step_x) % side) * side + (sy + step_y) % side) * 2 + sc)
            )
        return pairs

    swap = [(source, source ^ 1) for source in range(row_count)]

    def to_other_core(value):
        return lax.ppermute(value, "row", swap)

    mine = jnp.where(core == 0, activations, output_gradient)
    given = to_other_core(jnp.where(core == 0, output_gradient, activations))
    pair = jnp.concatenate(
        [jnp.where(core == 0, mine, given), jnp.where(core == 0, given, mine)], axis=0
    )
    slab = jnp.zeros((side,) + pair.shape, pair.dtype)
    slab = lax.dynamic_update_index_in_dim(slab, pair, first_at, 0)
    for step in (1, -1, 2):
        got = lax.ppermute(pair, "row", moves(step, 0))
        slab = lax.dynamic_update_index_in_dim(
            slab, got, lax.rem(first_at - step + side, side), 0
        )
    slab = slab.reshape(side * 2 * tokens, width)
    half = slab.shape[0] // 2

    before = lax.ppermute(slab, "row", moves(0, 1))
    after = lax.ppermute(slab, "row", moves(0, -1))
    far = jnp.concatenate(
        [
            lax.ppermute(before[:half], "row", moves(0, 1)),
            lax.ppermute(after[half:], "row", moves(0, -1)),
        ],
        axis=0,
    )
    gathered = jnp.zeros((2, side) + slab.shape, slab.dtype)
    for offset, part in ((0, slab), (-1, before), (1, after), (2, far)):
        for which, value, at in (
            (core, part, second_at),
            (1 - core, to_other_core(part), first_at),
        ):
            gathered = lax.dynamic_update_slice(
                gathered, value[None, None], (which, lax.rem(at + offset + side, side), 0, 0)
            )
    shape = (side, side, 2 * tokens, width)
    return gathered[0].reshape(shape), gathered[1].reshape(shape)


def body(
    activations,
    output_gradient,
    frozen_gate_weight,
    frozen_up_weight,
    frozen_down_weight,
    gate_adapter_first,
    gate_adapter_second,
    up_adapter_first,
    up_adapter_second,
    down_adapter_first,
    down_leave,
):
    share_tokens, width = activations.shape
    rank, hidden_units = gate_adapter_second.shape
    row_count = lax.axis_size("row")
    col_count = lax.axis_size("col")
    tokens_all = share_tokens * row_count
    col_tokens = tokens_all // col_count
    chips = row_count // 2
    core = lax.rem(lax.axis_index("row"), 2)
    cut = (hidden_units - rank) // 2
    wide_size = hidden_units - cut
    swap = [(i, i ^ 1) for i in range(row_count)]
    same_core = [[2 * chip + c for chip in range(chips)] for c in range(2)]

    gathered_act, gathered_out = gather_tokens(activations, output_gradient)
    side = gathered_act.shape[0]
    pair_tokens = 2 * share_tokens
    pairs_per_col = col_tokens // pair_tokens
    blocks_per_line = side // pairs_per_col
    full_act = gathered_act.reshape(tokens_all, width)
    full_out = gathered_out.reshape(tokens_all, width)

    def sum_over_col(gate_weight, up_weight, down_weight, up_steps):
        gate, up, back = lax.optimization_barrier(
            (
                multiply_right_transposed(full_act, gate_weight.T),
                multiply_right_transposed(full_act, up_weight.T),
                multiply_right_transposed(full_out, down_weight),
            )
        )

        def lines_block(partial, index):
            lines = partial.reshape(side, side, pair_tokens, -1)
            place = (lax.rem(index, blocks_per_line) * pairs_per_col, index // blocks_per_line)
            chosen = lax.dynamic_slice(
                lines, place + (0, 0), (pairs_per_col, 1, pair_tokens, lines.shape[3])
            )
            return chosen.reshape(col_tokens, -1)

        def block_of(index):
            return jnp.stack(
                [
                    lines_block(gate, index),
                    lines_block(up, index),
                    lax.dynamic_slice_in_dim(back, index * col_tokens, col_tokens, 0),
                ]
            )

        return ring_sum(block_of, "col", up_steps)

    def deltas_of(totals, low, columns):
        gate_activation = totals[0] + adapter_scale * matrix_multiply(
            low[0], gate_adapter_second[:, columns]
        )
        up_activation = totals[1] + adapter_scale * matrix_multiply(
            low[1], up_adapter_second[:, columns]
        )
        backward_result = totals[2] + adapter_scale * multiply_right_transposed(
            low[2], down_adapter_first[columns]
        )
        return pointwise(gate_activation, up_activation, backward_result)

    later = slice(cut, hidden_units)
    earlier = slice(0, cut)
    totals = sum_over_col(
        jnp.concatenate([frozen_gate_weight[:, later], gate_adapter_first], axis=1),
        jnp.concatenate([frozen_up_weight[:, later], up_adapter_first], axis=1),
        jnp.concatenate([frozen_down_weight[later], down_leave], axis=0),
        col_count // 2,
    )
    low = totals[:, :, wide_size:].astype(jnp.bfloat16)
    hidden, gate_delta, up_delta = deltas_of(totals[:, :, :wide_size], low, later)
    piece_later = ring_gather(
        jnp.concatenate([gate_delta, up_delta, hidden, low[0], low[1], low[2]], axis=1),
        "col",
        col_count // 2,
    )
    totals = sum_over_col(
        frozen_gate_weight[:, earlier],
        frozen_up_weight[:, earlier],
        frozen_down_weight[earlier],
        col_count - 1 - col_count // 2,
    )
    hidden, gate_delta, up_delta = deltas_of(totals, low, earlier)
    piece_earlier = ring_gather(
        jnp.concatenate([gate_delta, up_delta, hidden], axis=1),
        "col",
        col_count - 1 - col_count // 2,
    )

    pieces = ((piece_later, later, wide_size), (piece_earlier, earlier, cut))
    input_part = None
    factor_part = None
    for piece, columns, size in pieces:
        weight = jnp.concatenate(
            [frozen_gate_weight[:, columns], frozen_up_weight[:, columns]], axis=1
        )
        term = multiply_right_transposed(piece[:, : 2 * size], weight)
        input_part = term if input_part is None else input_part + term
        term = (
            multiply_right_transposed(piece[:, :size], gate_adapter_second[:, columns]),
            multiply_right_transposed(piece[:, size : 2 * size], up_adapter_second[:, columns]),
            matrix_multiply(piece[:, 2 * size : 3 * size], down_adapter_first[columns]),
        )
        factor_part = (
            term if factor_part is None else tuple(a + b for a, b in zip(factor_part, term))
        )
    gate_backward, up_backward, hidden_rank_product = [
        part.astype(jnp.bfloat16) for part in factor_part
    ]
    back_factors = jnp.concatenate([gate_backward, up_backward], axis=1)

    def sum_over_row(value):
        other = lax.dynamic_index_in_dim(value, 1 - core, 1, keepdims=False)
        own = lax.dynamic_index_in_dim(value, core, 1, keepdims=False)
        other = lax.ppermute(other, "row", swap)
        both = (own.astype(jnp.float32) + other.astype(jnp.float32)).astype(jnp.bfloat16)
        parts = lax.all_to_all(both, "row", 0, 0, axis_index_groups=same_core, tiled=True)
        return jnp.sum(parts.astype(jnp.float32), axis=0)

    features = width // row_count
    line_factors = back_factors.reshape(side, side, pair_tokens, 2 * rank)
    line_factors = line_factors.swapaxes(0, 1).reshape(tokens_all, 2 * rank)
    act_products = multiply_left_transposed(full_act, line_factors).astype(jnp.bfloat16)
    out_products = multiply_left_transposed(full_out, hidden_rank_product).astype(jnp.bfloat16)
    out_products = out_products.reshape(chips, 2, features, rank)
    products = jnp.concatenate(
        [
            act_products.reshape(chips, 2, features, 2 * rank),
            jnp.concatenate(
                [out_products[:, :, : features // 2], out_products[:, :, features // 2 :]], axis=3
            ),
        ],
        axis=2,
    )
    products = adapter_scale * sum_over_row(products)
    gate_adapter_first_gradient = products[:features, :rank]
    up_adapter_first_gradient = products[:features, rank:]
    down_adapter_second_gradient = jnp.concatenate(
        [products[features:, :rank], products[features:, rank:]], axis=0
    ).T

    share = jnp.concatenate([input_part.astype(jnp.bfloat16), back_factors], axis=1)
    summed = sum_over_row(share.reshape(chips, 2, share_tokens, width + 2 * rank))
    own_factors = summed[:, width:].astype(jnp.bfloat16)
    activation_gradient = (
        summed[:, :width]
        + adapter_scale
        * (
            multiply_right_transposed(own_factors[:, :rank], gate_adapter_first)
            + multiply_right_transposed(own_factors[:, rank:], up_adapter_first)
        )
    ).astype(jnp.bfloat16)

    lows = piece_later[:, 3 * wide_size :]
    gate_low, up_low, down_low = [lows[:, i * rank : (i + 1) * rank] for i in range(3)]

    def both_streams(take, axis):
        return adapter_scale * jnp.concatenate(
            [take(piece_earlier, cut), take(piece_later, wide_size)], axis=axis
        )

    gate_adapter_second_gradient = both_streams(
        lambda piece, size: multiply_left_transposed(gate_low, piece[:, :size]), 1
    )
    up_adapter_second_gradient = both_streams(
        lambda piece, size: multiply_left_transposed(up_low, piece[:, size : 2 * size]), 1
    )
    down_adapter_first_gradient = both_streams(
        lambda piece, size: multiply_left_transposed(piece[:, 2 * size : 3 * size], down_low), 0
    )
    return (
        activation_gradient,
        gate_adapter_first_gradient,
        gate_adapter_second_gradient,
        up_adapter_first_gradient,
        up_adapter_second_gradient,
        down_adapter_first_gradient,
        down_adapter_second_gradient,
    )


def solution(mesh):
    return jax.shard_map(
        body,
        mesh=mesh,
        in_specs=(
            P("row", "col"),
            P("row", "col"),
            P("col", "row"),
            P("col", "row"),
            P("row", "col"),
            P("col", None),
            P(None, "row"),
            P("col", None),
            P(None, "row"),
            P("row", None),
            P(None, "col"),
        ),
        out_specs=(
            P("row", "col"),
            P(("col", "row"), None),
            P(None, "row"),
            P(("col", "row"), None),
            P(None, "row"),
            P("row", None),
            P(None, ("col", "row")),
        ),
        check_vma=False,
    )
```

```python
import math

import jax
import jax.numpy as jnp
from jax import lax
from jax.sharding import PartitionSpec as P

adapter_scale = 0.5


def matrix_multiply(left, right):
    return jnp.dot(left, right, preferred_element_type=jnp.float32)


def multiply_right_transposed(left, right):
    return lax.dot_general(
        left, right, (((1,), (1,)), ((), ())), preferred_element_type=jnp.float32
    )


def multiply_left_transposed(left, right):
    return lax.dot_general(
        left, right, (((0,), (0,)), ((), ())), preferred_element_type=jnp.float32
    )


def pointwise(gate_activation, up_activation, backward_result):
    sigmoid_gate = jax.nn.sigmoid(gate_activation)
    silu_gate = gate_activation * sigmoid_gate
    hidden_state = (silu_gate * up_activation).astype(jnp.bfloat16)
    up_gradient_term = (backward_result * silu_gate).astype(jnp.bfloat16)
    gate_gradient_term = (
        backward_result
        * up_activation
        * sigmoid_gate
        * (1.0 + gate_activation * (1.0 - sigmoid_gate))
    ).astype(jnp.bfloat16)
    return (hidden_state, gate_gradient_term, up_gradient_term)


def shifted(size, step):
    return [(i, (i + step) % size) for i in range(size)]


def two_way_rings(axis, operands, up_steps, arrive):
    size = lax.axis_size(axis)
    state = list(operands)
    for step in range(1, size // 2 + 1):
        for stream, steps in enumerate(up_steps):
            up, down = state[stream]
            if step <= steps:
                up = lax.ppermute(up, axis, shifted(size, 1))
            if step <= size - 1 - steps:
                down = lax.ppermute(down, axis, shifted(size, -1))
            state[stream] = arrive(stream, step, up, down)
    return state


def ring_sums(block_ofs, axis, up_steps, operands):
    size = lax.axis_size(axis)
    here = lax.axis_index(axis)

    def block(stream, offset):
        return block_ofs[stream](lax.rem(here + offset + size, size))

    def arrive(stream, step, up, down):
        ups = up_steps[stream]
        downs = size - 1 - ups
        if step < ups:
            up = (up.astype(jnp.float32) + block(stream, ups - step)).astype(jnp.bfloat16)
        if step < downs:
            down = (down.astype(jnp.float32) + block(stream, step - downs)).astype(jnp.bfloat16)
        return up, down

    return [
        up.astype(jnp.float32) + down.astype(jnp.float32) + block(stream, 0)
        for stream, (up, down) in enumerate(two_way_rings(axis, operands, up_steps, arrive))
    ]


def ring_gathers(blocks, axis, up_steps):
    size = lax.axis_size(axis)
    here = lax.axis_index(axis)
    gathered = [
        lax.dynamic_update_index_in_dim(
            jnp.zeros((size,) + block.shape, block.dtype), block, here, 0
        )
        for block in blocks
    ]
    arrivals = []

    def arrive(stream, step, up, down):
        if step <= up_steps[stream]:
            gathered[stream] = lax.dynamic_update_index_in_dim(
                gathered[stream], up, lax.rem(here - step + size, size), 0
            )
            if stream == 0:
                arrivals.append(up)
        if step <= size - 1 - up_steps[stream]:
            gathered[stream] = lax.dynamic_update_index_in_dim(
                gathered[stream], down, lax.rem(here + step, size), 0
            )
        return up, down

    two_way_rings(axis, [(block, block) for block in blocks], up_steps, arrive)
    pieces = [
        whole.reshape((size * block.shape[0],) + block.shape[1:])
        for whole, block in zip(gathered, blocks)
    ]
    return pieces, arrivals


def gather_tokens(activations, output_gradient):
    tokens, width = activations.shape
    row_count = lax.axis_size("row")
    side = math.isqrt(row_count // 2)
    here = lax.axis_index("row")
    core = lax.rem(here, 2)
    x = here // (2 * side)
    y = lax.rem(here // 2, side)
    first_at = jnp.where(core == 0, x, y)
    second_at = jnp.where(core == 0, y, x)

    def moves(first, second):
        pairs = []
        for source in range(row_count):
            sx, sy, sc = source // (2 * side), source // 2 % side, source % 2
            step_x, step_y = (first, second) if sc == 0 else (second, first)
            pairs.append(
                (source, (((sx + step_x) % side) * side + (sy + step_y) % side) * 2 + sc)
            )
        return pairs

    swap = [(source, source ^ 1) for source in range(row_count)]

    def to_other_core(value):
        return lax.ppermute(value, "row", swap)

    mine = jnp.where(core == 0, activations, output_gradient)
    given = to_other_core(jnp.where(core == 0, output_gradient, activations))
    pair = jnp.concatenate(
        [jnp.where(core == 0, mine, given), jnp.where(core == 0, given, mine)], axis=0
    )
    slab = jnp.zeros((side,) + pair.shape, pair.dtype)
    slab = lax.dynamic_update_index_in_dim(slab, pair, first_at, 0)
    for step in (1, -1, 2):
        got = lax.ppermute(pair, "row", moves(step, 0))
        slab = lax.dynamic_update_index_in_dim(
            slab, got, lax.rem(first_at - step + side, side), 0
        )
    slab = slab.reshape(side * 2 * tokens, width)
    half = slab.shape[0] // 2

    before = lax.ppermute(slab, "row", moves(0, 1))
    after = lax.ppermute(slab, "row", moves(0, -1))
    far = jnp.concatenate(
        [
            lax.ppermute(before[:half], "row", moves(0, 1)),
            lax.ppermute(after[half:], "row", moves(0, -1)),
        ],
        axis=0,
    )
    gathered = jnp.zeros((2, side) + slab.shape, slab.dtype)
    for offset, part in ((0, slab), (-1, before), (1, after), (2, far)):
        for which, value, at in (
            (core, part, second_at),
            (1 - core, to_other_core(part), first_at),
        ):
            gathered = lax.dynamic_update_slice(
                gathered, value[None, None], (which, lax.rem(at + offset + side, side), 0, 0)
            )
    shape = (side, side, 2 * tokens, width)
    return gathered[0].reshape(shape), gathered[1].reshape(shape)


def body(
    activations,
    output_gradient,
    frozen_gate_weight,
    frozen_up_weight,
    frozen_down_weight,
    gate_adapter_first,
    gate_adapter_second,
    up_adapter_first,
    up_adapter_second,
    down_adapter_first,
    down_leave,
):
    share_tokens, width = activations.shape
    rank, hidden_units = gate_adapter_second.shape
    row_count = lax.axis_size("row")
    col_count = lax.axis_size("col")
    tokens_all = share_tokens * row_count
    col_tokens = tokens_all // col_count
    chips = row_count // 2
    core = lax.rem(lax.axis_index("row"), 2)
    cut = (hidden_units - rank) // 2
    wide_size = hidden_units - cut
    swap = [(i, i ^ 1) for i in range(row_count)]
    same_core = [[2 * chip + c for chip in range(chips)] for c in range(2)]

    gathered_act, gathered_out = gather_tokens(activations, output_gradient)
    side = gathered_act.shape[0]
    pair_tokens = 2 * share_tokens
    pairs_per_col = col_tokens // pair_tokens
    blocks_per_line = side // pairs_per_col
    full_act = gathered_act.reshape(tokens_all, width)
    full_out = gathered_out.reshape(tokens_all, width)

    def partials_of(act, out, gate_weight, up_weight, down_weight):
        return lax.optimization_barrier(
            (
                multiply_right_transposed(act, gate_weight.T),
                multiply_right_transposed(act, up_weight.T),
                multiply_right_transposed(out, down_weight),
            )
        )

    def blocks_of(partials):
        gate, up, back = partials

        def lines_block(partial, index):
            lines = partial.reshape(side, side, pair_tokens, -1)
            place = (lax.rem(index, blocks_per_line) * pairs_per_col, index // blocks_per_line)
            chosen = lax.dynamic_slice(
                lines, place + (0, 0), (pairs_per_col, 1, pair_tokens, lines.shape[3])
            )
            return chosen.reshape(col_tokens, -1)

        def block_of(index):
            return jnp.stack(
                [
                    lines_block(gate, index),
                    lines_block(up, index),
                    lax.dynamic_slice_in_dim(back, index * col_tokens, col_tokens, 0),
                ]
            )

        return block_of

    def first_operands(block_of, ups):
        here = lax.axis_index("col")
        return tuple(
            block_of(lax.rem(here + offset + col_count, col_count)).astype(jnp.bfloat16)
            for offset in (ups, ups + 1 - col_count)
        )

    def deltas_of(totals, low, columns):
        gate_activation = totals[0] + adapter_scale * matrix_multiply(
            low[0], gate_adapter_second[:, columns]
        )
        up_activation = totals[1] + adapter_scale * matrix_multiply(
            low[1], up_adapter_second[:, columns]
        )
        backward_result = totals[2] + adapter_scale * multiply_right_transposed(
            low[2], down_adapter_first[columns]
        )
        return pointwise(gate_activation, up_activation, backward_result)

    later = slice(cut, hidden_units)
    earlier = slice(0, cut)
    first_partials = partials_of(
        full_act,
        full_out,
        jnp.concatenate([frozen_gate_weight[:, later], gate_adapter_first], axis=1),
        jnp.concatenate([frozen_up_weight[:, later], up_adapter_first], axis=1),
        jnp.concatenate([frozen_down_weight[later], down_leave], axis=0),
    )
    up_steps = (col_count // 2, col_count - 1 - col_count // 2)
    first_blocks = blocks_of(first_partials)
    first_sent = first_operands(first_blocks, up_steps[0])
    act_after, out_after = lax.optimization_barrier((full_act, full_out) + first_sent)[:2]
    second_partials = partials_of(
        act_after,
        out_after,
        frozen_gate_weight[:, earlier],
        frozen_up_weight[:, earlier],
        frozen_down_weight[earlier],
    )
    second_blocks = blocks_of(second_partials)
    totals, second_totals = ring_sums(
        (first_blocks, second_blocks),
        "col",
        up_steps,
        (first_sent, first_operands(second_blocks, up_steps[1])),
    )
    low = totals[:, :, wide_size:].astype(jnp.bfloat16)
    later_deltas = deltas_of(totals[:, :, :wide_size], low, later)
    earlier_deltas = deltas_of(second_totals, low, earlier)

    own_factors = None
    for (hidden, gate_delta, up_delta), columns in (
        (later_deltas, later),
        (earlier_deltas, earlier),
    ):
        term = jnp.concatenate(
            [
                matrix_multiply(hidden, down_adapter_first[columns]),
                multiply_right_transposed(gate_delta, gate_adapter_second[:, columns]),
                multiply_right_transposed(up_delta, up_adapter_second[:, columns]),
            ],
            axis=1,
        )
        own_factors = term if own_factors is None else own_factors + term

    def to_all(value, axis):
        count = lax.axis_size(axis)
        return lax.all_to_all(
            jnp.broadcast_to(value[None], (count,) + value.shape), axis, 0, 0, tiled=True
        )

    later_block = jnp.concatenate(
        [later_deltas[1], later_deltas[2], later_deltas[0], low[0], low[1], low[2]], axis=1
    )
    earlier_block = jnp.concatenate(
        [earlier_deltas[1], earlier_deltas[2], earlier_deltas[0]], axis=1
    )
    (piece_later, piece_earlier), arrivals = ring_gathers(
        (later_block, earlier_block), "col", up_steps
    )
    factor_parts = to_all(own_factors.astype(jnp.bfloat16), "row")
    factor_parts = lax.optimization_barrier((factor_parts, arrivals[1]))[0]
    own_factors = jnp.sum(factor_parts.astype(jnp.float32), axis=0).astype(jnp.bfloat16)
    factors = to_all(own_factors, "col").reshape(tokens_all, 3 * rank)

    streams = []
    for piece, columns, size in (
        (piece_later, later, wide_size),
        (piece_earlier, earlier, cut),
    ):
        weight = lax.optimization_barrier(
            jnp.concatenate([frozen_gate_weight[:, columns], frozen_up_weight[:, columns]], axis=1)
        )
        deltas = piece[:, : 2 * size].reshape(chips, 2, share_tokens, 2 * size)
        streams.append((deltas, weight))

    def input_part(which):
        terms = [
            multiply_right_transposed(
                lax.dynamic_index_in_dim(deltas, which, 1, keepdims=False).reshape(
                    chips * share_tokens, -1
                ),
                weight,
            )
            for deltas, weight in streams
        ]
        return terms[0] + terms[1]

    other = lax.ppermute(input_part(1 - core).astype(jnp.bfloat16), "row", swap)
    share = (input_part(core) + other.astype(jnp.float32)).astype(jnp.bfloat16)
    shares = lax.all_to_all(share, "row", 0, 0, axis_index_groups=same_core, tiled=True)
    summed = jnp.sum(shares.reshape(chips, share_tokens, width).astype(jnp.float32), axis=0)

    first_token = lax.axis_index("row") * share_tokens
    row_factors = lax.dynamic_slice_in_dim(factors, first_token, share_tokens, 0)
    activation_gradient = (
        summed
        + adapter_scale
        * (
            multiply_right_transposed(row_factors[:, rank : 2 * rank], gate_adapter_first)
            + multiply_right_transposed(row_factors[:, 2 * rank :], up_adapter_first)
        )
    ).astype(jnp.bfloat16)

    features = width // row_count
    first_feature = lax.axis_index("row") * features
    activation_columns = lax.dynamic_slice_in_dim(full_act, first_feature, features, 1)
    activation_columns = activation_columns.reshape(side, side, pair_tokens, features)
    activation_columns = activation_columns.swapaxes(0, 1).reshape(tokens_all, features)
    output_columns = lax.dynamic_slice_in_dim(full_out, first_feature, features, 1)
    first_gradients = adapter_scale * multiply_left_transposed(
        activation_columns, factors[:, rank:]
    )
    gate_adapter_first_gradient = first_gradients[:, :rank]
    up_adapter_first_gradient = first_gradients[:, rank:]
    down_adapter_second_gradient = adapter_scale * multiply_left_transposed(
        factors[:, :rank], output_columns
    )

    lows = piece_later[:, 3 * wide_size :]
    gate_low, up_low, down_low = [lows[:, i * rank : (i + 1) * rank] for i in range(3)]

    def both_streams(take, axis):
        return adapter_scale * jnp.concatenate(
            [take(piece_earlier, cut), take(piece_later, wide_size)], axis=axis
        )

    gate_adapter_second_gradient = both_streams(
        lambda piece, size: multiply_left_transposed(gate_low, piece[:, :size]), 1
    )
    up_adapter_second_gradient = both_streams(
        lambda piece, size: multiply_left_transposed(up_low, piece[:, size : 2 * size]), 1
    )
    down_adapter_first_gradient = both_streams(
        lambda piece, size: multiply_left_transposed(piece[:, 2 * size : 3 * size], down_low), 0
    )
    return (
        activation_gradient,
        gate_adapter_first_gradient,
        gate_adapter_second_gradient,
        up_adapter_first_gradient,
        up_adapter_second_gradient,
        down_adapter_first_gradient,
        down_adapter_second_gradient,
    )


def solution(mesh):
    return jax.shard_map(
        body,
        mesh=mesh,
        in_specs=(
            P("row", "col"),
            P("row", "col"),
            P("col", "row"),
            P("col", "row"),
            P("row", "col"),
            P("col", None),
            P(None, "row"),
            P("col", None),
            P(None, "row"),
            P("row", None),
            P(None, "col"),
        ),
        out_specs=(
            P("row", "col"),
            P(("col", "row"), None),
            P(None, "row"),
            P(("col", "row"), None),
            P(None, "row"),
            P("row", None),
            P(None, ("col", "row")),
        ),
        check_vma=False,
    )
```

```python
import math

import jax
import jax.numpy as jnp
from jax import lax
from jax.sharding import PartitionSpec as P

adapter_scale = 0.5


def matrix_multiply(left, right):
    return jnp.dot(left, right, preferred_element_type=jnp.float32)


def multiply_right_transposed(left, right):
    return lax.dot_general(
        left, right, (((1,), (1,)), ((), ())), preferred_element_type=jnp.float32
    )


def multiply_left_transposed(left, right):
    return lax.dot_general(
        left, right, (((0,), (0,)), ((), ())), preferred_element_type=jnp.float32
    )


def pointwise(gate_activation, up_activation, backward_result):
    sigmoid_gate = jax.nn.sigmoid(gate_activation)
    silu_gate = gate_activation * sigmoid_gate
    hidden_state = (silu_gate * up_activation).astype(jnp.bfloat16)
    up_gradient_term = (backward_result * silu_gate).astype(jnp.bfloat16)
    gate_gradient_term = (
        backward_result
        * up_activation
        * sigmoid_gate
        * (1.0 + gate_activation * (1.0 - sigmoid_gate))
    ).astype(jnp.bfloat16)
    return (hidden_state, gate_gradient_term, up_gradient_term)


def shifted(size, step):
    return [(i, (i + step) % size) for i in range(size)]


def two_way_rings(axis, operands, up_steps, arrive):
    size = lax.axis_size(axis)
    state = list(operands)
    for step in range(1, size // 2 + 1):
        for stream, steps in enumerate(up_steps):
            up, down = state[stream]
            if step <= steps:
                up = lax.ppermute(up, axis, shifted(size, 1))
            if step <= size - 1 - steps:
                down = lax.ppermute(down, axis, shifted(size, -1))
            state[stream] = arrive(stream, step, up, down)
    return state


def ring_sums(block_ofs, axis, up_steps, operands):
    size = lax.axis_size(axis)
    here = lax.axis_index(axis)

    def block(stream, offset):
        return block_ofs[stream](lax.rem(here + offset + size, size))

    def arrive(stream, step, up, down):
        ups = up_steps[stream]
        downs = size - 1 - ups
        if step < ups:
            up = (up.astype(jnp.float32) + block(stream, ups - step)).astype(jnp.bfloat16)
        if step < downs:
            down = (down.astype(jnp.float32) + block(stream, step - downs)).astype(jnp.bfloat16)
        return up, down

    return [
        up.astype(jnp.float32) + down.astype(jnp.float32) + block(stream, 0)
        for stream, (up, down) in enumerate(two_way_rings(axis, operands, up_steps, arrive))
    ]


def gather_tokens(activations, output_gradient):
    tokens, width = activations.shape
    row_count = lax.axis_size("row")
    side = math.isqrt(row_count // 2)
    here = lax.axis_index("row")
    core = lax.rem(here, 2)
    x = here // (2 * side)
    y = lax.rem(here // 2, side)
    first_at = jnp.where(core == 0, x, y)
    second_at = jnp.where(core == 0, y, x)

    def moves(first, second):
        pairs = []
        for source in range(row_count):
            sx, sy, sc = source // (2 * side), source // 2 % side, source % 2
            step_x, step_y = (first, second) if sc == 0 else (second, first)
            pairs.append(
                (source, (((sx + step_x) % side) * side + (sy + step_y) % side) * 2 + sc)
            )
        return pairs

    swap = [(source, source ^ 1) for source in range(row_count)]

    def to_other_core(value):
        return lax.ppermute(value, "row", swap)

    mine = jnp.where(core == 0, activations, output_gradient)
    given = to_other_core(jnp.where(core == 0, output_gradient, activations))
    pair = jnp.concatenate(
        [jnp.where(core == 0, mine, given), jnp.where(core == 0, given, mine)], axis=0
    )
    slab = jnp.zeros((side,) + pair.shape, pair.dtype)
    slab = lax.dynamic_update_index_in_dim(slab, pair, first_at, 0)
    for step in (1, -1, 2):
        got = lax.ppermute(pair, "row", moves(step, 0))
        slab = lax.dynamic_update_index_in_dim(
            slab, got, lax.rem(first_at - step + side, side), 0
        )
    slab = slab.reshape(side * 2 * tokens, width)
    half = slab.shape[0] // 2

    before = lax.ppermute(slab, "row", moves(0, 1))
    after = lax.ppermute(slab, "row", moves(0, -1))
    far = jnp.concatenate(
        [
            lax.ppermute(before[:half], "row", moves(0, 1)),
            lax.ppermute(after[half:], "row", moves(0, -1)),
        ],
        axis=0,
    )
    gathered = jnp.zeros((2, side) + slab.shape, slab.dtype)
    for offset, part in ((0, slab), (-1, before), (1, after), (2, far)):
        for which, value, at in (
            (core, part, second_at),
            (1 - core, to_other_core(part), first_at),
        ):
            gathered = lax.dynamic_update_slice(
                gathered, value[None, None], (which, lax.rem(at + offset + side, side), 0, 0)
            )
    shape = (side, side, 2 * tokens, width)
    return gathered[0].reshape(shape), gathered[1].reshape(shape)


def body(
    activations,
    output_gradient,
    frozen_gate_weight,
    frozen_up_weight,
    frozen_down_weight,
    gate_adapter_first,
    gate_adapter_second,
    up_adapter_first,
    up_adapter_second,
    down_adapter_first,
    down_leave,
):
    share_tokens, width = activations.shape
    rank, hidden_units = gate_adapter_second.shape
    row_count = lax.axis_size("row")
    col_count = lax.axis_size("col")
    tokens_all = share_tokens * row_count
    col_tokens = tokens_all // col_count
    chips = row_count // 2
    core = lax.rem(lax.axis_index("row"), 2)
    cut = (hidden_units - rank) // 2
    wide_size = hidden_units - cut
    swap = [(i, i ^ 1) for i in range(row_count)]
    same_core = [[2 * chip + c for chip in range(chips)] for c in range(2)]

    gathered_act, gathered_out = gather_tokens(activations, output_gradient)
    side = gathered_act.shape[0]
    pair_tokens = 2 * share_tokens
    pairs_per_col = col_tokens // pair_tokens
    blocks_per_line = side // pairs_per_col
    full_act = gathered_act.reshape(tokens_all, width)
    full_out = gathered_out.reshape(tokens_all, width)

    def blocks_of(first, size):
        def lines_block(partial, index):
            lines = partial.reshape(side, side, pair_tokens, -1)
            place = (lax.rem(index, blocks_per_line) * pairs_per_col, index // blocks_per_line)
            chosen = lax.dynamic_slice(
                lines, place + (0, first), (pairs_per_col, 1, pair_tokens, size)
            )
            return chosen.reshape(col_tokens, size)

        def block_of(index):
            return jnp.stack(
                [
                    lines_block(partials[0], index),
                    lines_block(partials[1], index),
                    lax.dynamic_slice(
                        partials[2], (index * col_tokens, first), (col_tokens, size)
                    ),
                ]
            )

        return block_of

    def first_operands(block_of, ups):
        here = lax.axis_index("col")
        return tuple(
            block_of(lax.rem(here + offset + col_count, col_count)).astype(jnp.bfloat16)
            for offset in (ups, ups + 1 - col_count)
        )

    def deltas_of(totals, low, columns):
        gate_activation = totals[0] + adapter_scale * matrix_multiply(
            low[0], gate_adapter_second[:, columns]
        )
        up_activation = totals[1] + adapter_scale * matrix_multiply(
            low[1], up_adapter_second[:, columns]
        )
        backward_result = totals[2] + adapter_scale * multiply_right_transposed(
            low[2], down_adapter_first[columns]
        )
        return pointwise(gate_activation, up_activation, backward_result)

    partials = lax.optimization_barrier(
        (
            multiply_right_transposed(
                full_act, jnp.concatenate([frozen_gate_weight, gate_adapter_first], axis=1).T
            ),
            multiply_right_transposed(
                full_act, jnp.concatenate([frozen_up_weight, up_adapter_first], axis=1).T
            ),
            multiply_right_transposed(
                full_out, jnp.concatenate([frozen_down_weight, down_leave], axis=0)
            ),
        )
    )
    later = slice(cut, hidden_units)
    earlier = slice(0, cut)
    up_steps = (col_count // 2, col_count - 1 - col_count // 2)
    block_ofs = (blocks_of(cut, wide_size + rank), blocks_of(0, cut))
    totals, second_totals = ring_sums(
        block_ofs,
        "col",
        up_steps,
        [first_operands(block_of, ups) for block_of, ups in zip(block_ofs, up_steps)],
    )
    low = totals[:, :, wide_size:].astype(jnp.bfloat16)
    later_deltas = deltas_of(totals[:, :, :wide_size], low, later)
    earlier_deltas = deltas_of(second_totals, low, earlier)

    own_factors = None
    for (hidden, gate_delta, up_delta), columns in (
        (later_deltas, later),
        (earlier_deltas, earlier),
    ):
        term = jnp.concatenate(
            [
                matrix_multiply(hidden, down_adapter_first[columns]),
                multiply_right_transposed(gate_delta, gate_adapter_second[:, columns]),
                multiply_right_transposed(up_delta, up_adapter_second[:, columns]),
            ],
            axis=1,
        )
        own_factors = term if own_factors is None else own_factors + term

    def to_all(value, axis):
        count = lax.axis_size(axis)
        return lax.all_to_all(
            jnp.broadcast_to(value[None], (count,) + value.shape), axis, 0, 0, tiled=True
        )

    packed = jnp.concatenate(
        [
            earlier_deltas[1],
            later_deltas[1],
            earlier_deltas[2],
            later_deltas[2],
            earlier_deltas[0],
            later_deltas[0],
            low[0],
            low[1],
            low[2],
        ],
        axis=1,
    )
    piece = lax.all_gather(packed, "col", axis=0, tiled=True)
    factor_parts = to_all(own_factors.astype(jnp.bfloat16), "row")
    own_factors = jnp.sum(factor_parts.astype(jnp.float32), axis=0).astype(jnp.bfloat16)
    factors = to_all(own_factors, "col").reshape(tokens_all, 3 * rank)
    gate_weight, up_weight = lax.optimization_barrier(
        (frozen_gate_weight, frozen_up_weight, packed)
    )[:2]
    input_weight = jnp.concatenate([gate_weight, up_weight], axis=1)
    piece, factors, input_weight = lax.optimization_barrier((piece, factors, input_weight))

    deltas = piece[:, : 2 * hidden_units].reshape(chips, 2, share_tokens, 2 * hidden_units)

    def input_part(which):
        chosen = lax.dynamic_index_in_dim(deltas, which, 1, keepdims=False)
        return multiply_right_transposed(
            chosen.reshape(chips * share_tokens, 2 * hidden_units), input_weight
        )

    other = lax.ppermute(input_part(1 - core).astype(jnp.bfloat16), "row", swap)
    share = (input_part(core) + other.astype(jnp.float32)).astype(jnp.bfloat16)
    shares = lax.all_to_all(share, "row", 0, 0, axis_index_groups=same_core, tiled=True)
    summed = jnp.sum(shares.reshape(chips, share_tokens, width).astype(jnp.float32), axis=0)

    first_token = lax.axis_index("row") * share_tokens
    row_factors = lax.dynamic_slice_in_dim(factors, first_token, share_tokens, 0)
    activation_gradient = (
        summed
        + adapter_scale
        * (
            multiply_right_transposed(row_factors[:, rank : 2 * rank], gate_adapter_first)
            + multiply_right_transposed(row_factors[:, 2 * rank :], up_adapter_first)
        )
    ).astype(jnp.bfloat16)

    features = width // row_count
    first_feature = lax.axis_index("row") * features
    activation_columns = lax.dynamic_slice_in_dim(full_act, first_feature, features, 1)
    activation_columns = activation_columns.reshape(side, side, pair_tokens, features)
    activation_columns = activation_columns.swapaxes(0, 1).reshape(tokens_all, features)
    output_columns = lax.dynamic_slice_in_dim(full_out, first_feature, features, 1)
    first_gradients = adapter_scale * multiply_left_transposed(
        activation_columns, factors[:, rank:]
    )
    gate_adapter_first_gradient = first_gradients[:, :rank]
    up_adapter_first_gradient = first_gradients[:, rank:]
    down_adapter_second_gradient = adapter_scale * multiply_left_transposed(
        factors[:, :rank], output_columns
    )

    piece_gate = piece[:, :hidden_units]
    piece_up = piece[:, hidden_units : 2 * hidden_units]
    piece_hidden = piece[:, 2 * hidden_units : 3 * hidden_units]
    lows = piece[:, 3 * hidden_units :]
    gate_low, up_low, down_low = [lows[:, i * rank : (i + 1) * rank] for i in range(3)]
    gate_adapter_second_gradient = adapter_scale * multiply_left_transposed(gate_low, piece_gate)
    up_adapter_second_gradient = adapter_scale * multiply_left_transposed(up_low, piece_up)
    down_adapter_first_gradient = adapter_scale * multiply_left_transposed(piece_hidden, down_low)
    return (
        activation_gradient,
        gate_adapter_first_gradient,
        gate_adapter_second_gradient,
        up_adapter_first_gradient,
        up_adapter_second_gradient,
        down_adapter_first_gradient,
        down_adapter_second_gradient,
    )


def solution(mesh):
    return jax.shard_map(
        body,
        mesh=mesh,
        in_specs=(
            P("row", "col"),
            P("row", "col"),
            P("col", "row"),
            P("col", "row"),
            P("row", "col"),
            P("col", None),
            P(None, "row"),
            P("col", None),
            P(None, "row"),
            P("row", None),
            P(None, "col"),
        ),
        out_specs=(
            P("row", "col"),
            P(("col", "row"), None),
            P(None, "row"),
            P(("col", "row"), None),
            P(None, "row"),
            P("row", None),
            P(None, ("col", "row")),
        ),
        check_vma=False,
    )
```

```python
import math

import jax
import jax.numpy as jnp
from jax import lax
from jax.sharding import PartitionSpec as P

adapter_scale = 0.5


def matrix_multiply(left, right):
    return jnp.dot(left, right, preferred_element_type=jnp.float32)


def multiply_right_transposed(left, right):
    return lax.dot_general(
        left, right, (((1,), (1,)), ((), ())), preferred_element_type=jnp.float32
    )


def multiply_left_transposed(left, right):
    return lax.dot_general(
        left, right, (((0,), (0,)), ((), ())), preferred_element_type=jnp.float32
    )


def pointwise(gate_activation, up_activation, backward_result):
    sigmoid_gate = jax.nn.sigmoid(gate_activation)
    silu_gate = gate_activation * sigmoid_gate
    hidden_state = (silu_gate * up_activation).astype(jnp.bfloat16)
    up_gradient_term = (backward_result * silu_gate).astype(jnp.bfloat16)
    gate_gradient_term = (
        backward_result
        * up_activation
        * sigmoid_gate
        * (1.0 + gate_activation * (1.0 - sigmoid_gate))
    ).astype(jnp.bfloat16)
    return (hidden_state, gate_gradient_term, up_gradient_term)


def shifted(size, step):
    return [(i, (i + step) % size) for i in range(size)]


def two_way_rings(axis, operands, up_steps, arrive):
    size = lax.axis_size(axis)
    state = list(operands)
    for step in range(1, size // 2 + 1):
        for stream, steps in enumerate(up_steps):
            up, down = state[stream]
            if step <= steps:
                up = lax.ppermute(up, axis, shifted(size, 1))
            if step <= size - 1 - steps:
                down = lax.ppermute(down, axis, shifted(size, -1))
            state[stream] = arrive(stream, step, up, down)
    return state


def ring_sums(block_ofs, axis, up_steps, operands):
    size = lax.axis_size(axis)
    here = lax.axis_index(axis)

    def block(stream, offset):
        return block_ofs[stream](lax.rem(here + offset + size, size))

    def arrive(stream, step, up, down):
        ups = up_steps[stream]
        downs = size - 1 - ups
        if step < ups:
            up = (up.astype(jnp.float32) + block(stream, ups - step)).astype(jnp.bfloat16)
        if step < downs:
            down = (down.astype(jnp.float32) + block(stream, step - downs)).astype(jnp.bfloat16)
        return up, down

    return [
        up.astype(jnp.float32) + down.astype(jnp.float32) + block(stream, 0)
        for stream, (up, down) in enumerate(two_way_rings(axis, operands, up_steps, arrive))
    ]


def gather_tokens(activations, output_gradient):
    tokens, width = activations.shape
    row_count = lax.axis_size("row")
    side = math.isqrt(row_count // 2)
    here = lax.axis_index("row")
    core = lax.rem(here, 2)
    x = here // (2 * side)
    y = lax.rem(here // 2, side)
    first_at = jnp.where(core == 0, x, y)
    second_at = jnp.where(core == 0, y, x)

    def moves(first, second):
        pairs = []
        for source in range(row_count):
            sx, sy, sc = source // (2 * side), source // 2 % side, source % 2
            step_x, step_y = (first, second) if sc == 0 else (second, first)
            pairs.append(
                (source, (((sx + step_x) % side) * side + (sy + step_y) % side) * 2 + sc)
            )
        return pairs

    swap = [(source, source ^ 1) for source in range(row_count)]

    def to_other_core(value):
        return lax.ppermute(value, "row", swap)

    mine = jnp.where(core == 0, activations, output_gradient)
    given = to_other_core(jnp.where(core == 0, output_gradient, activations))
    pair = jnp.concatenate(
        [jnp.where(core == 0, mine, given), jnp.where(core == 0, given, mine)], axis=0
    )
    slab = jnp.zeros((side,) + pair.shape, pair.dtype)
    slab = lax.dynamic_update_index_in_dim(slab, pair, first_at, 0)
    for step in (1, -1, 2):
        got = lax.ppermute(pair, "row", moves(step, 0))
        slab = lax.dynamic_update_index_in_dim(
            slab, got, lax.rem(first_at - step + side, side), 0
        )
    slab = slab.reshape(side * 2 * tokens, width)
    half = slab.shape[0] // 2

    before = lax.ppermute(slab, "row", moves(0, 1))
    after = lax.ppermute(slab, "row", moves(0, -1))
    far = jnp.concatenate(
        [
            lax.ppermute(slab[:half], "row", moves(0, 2)),
            lax.ppermute(slab[half:], "row", moves(0, -2)),
        ],
        axis=0,
    )
    gathered = jnp.zeros((2, side) + slab.shape, slab.dtype)
    for offset, part in ((0, slab), (-1, before), (1, after), (2, far)):
        for which, value, at in (
            (core, part, second_at),
            (1 - core, to_other_core(part), first_at),
        ):
            gathered = lax.dynamic_update_slice(
                gathered, value[None, None], (which, lax.rem(at + offset + side, side), 0, 0)
            )
    shape = (side, side, 2 * tokens, width)
    return gathered[0].reshape(shape), gathered[1].reshape(shape)


def body(
    activations,
    output_gradient,
    frozen_gate_weight,
    frozen_up_weight,
    frozen_down_weight,
    gate_adapter_first,
    gate_adapter_second,
    up_adapter_first,
    up_adapter_second,
    down_adapter_first,
    down_leave,
):
    share_tokens, width = activations.shape
    rank, hidden_units = gate_adapter_second.shape
    row_count = lax.axis_size("row")
    col_count = lax.axis_size("col")
    tokens_all = share_tokens * row_count
    col_tokens = tokens_all // col_count
    chips = row_count // 2
    core = lax.rem(lax.axis_index("row"), 2)
    cut = (hidden_units - rank) // 2
    wide_size = hidden_units - cut
    swap = [(i, i ^ 1) for i in range(row_count)]
    same_core = [[2 * chip + c for chip in range(chips)] for c in range(2)]

    gathered_act, gathered_out = gather_tokens(activations, output_gradient)
    side = gathered_act.shape[0]
    pair_tokens = 2 * share_tokens
    pairs_per_col = col_tokens // pair_tokens
    blocks_per_line = side // pairs_per_col
    full_act = gathered_act.reshape(tokens_all, width)
    full_out = gathered_out.reshape(tokens_all, width)

    def blocks_of(first, size):
        def lines_block(partial, index):
            lines = partial.reshape(side, side, pair_tokens, -1)
            place = (lax.rem(index, blocks_per_line) * pairs_per_col, index // blocks_per_line)
            chosen = lax.dynamic_slice(
                lines, place + (0, first), (pairs_per_col, 1, pair_tokens, size)
            )
            return chosen.reshape(col_tokens, size)

        def block_of(index):
            return jnp.stack(
                [
                    lines_block(partials[0], index),
                    lines_block(partials[1], index),
                    lax.dynamic_slice(
                        partials[2], (index * col_tokens, first), (col_tokens, size)
                    ),
                ]
            )

        return block_of

    def first_operands(block_of, ups):
        here = lax.axis_index("col")
        return tuple(
            block_of(lax.rem(here + offset + col_count, col_count)).astype(jnp.bfloat16)
            for offset in (ups, ups + 1 - col_count)
        )

    def deltas_of(totals, low, columns):
        gate_activation = totals[0] + adapter_scale * matrix_multiply(
            low[0], gate_adapter_second[:, columns]
        )
        up_activation = totals[1] + adapter_scale * matrix_multiply(
            low[1], up_adapter_second[:, columns]
        )
        backward_result = totals[2] + adapter_scale * multiply_right_transposed(
            low[2], down_adapter_first[columns]
        )
        return pointwise(gate_activation, up_activation, backward_result)

    partials = lax.optimization_barrier(
        (
            multiply_right_transposed(
                full_act, jnp.concatenate([frozen_gate_weight, gate_adapter_first], axis=1).T
            ),
            multiply_right_transposed(
                full_act, jnp.concatenate([frozen_up_weight, up_adapter_first], axis=1).T
            ),
            multiply_right_transposed(
                full_out, jnp.concatenate([frozen_down_weight, down_leave], axis=0)
            ),
        )
    )
    later = slice(cut, hidden_units)
    earlier = slice(0, cut)
    up_steps = (col_count // 2, col_count - 1 - col_count // 2)
    block_ofs = (blocks_of(cut, wide_size + rank), blocks_of(0, cut))
    totals, second_totals = ring_sums(
        block_ofs,
        "col",
        up_steps,
        [first_operands(block_of, ups) for block_of, ups in zip(block_ofs, up_steps)],
    )
    low = totals[:, :, wide_size:].astype(jnp.bfloat16)
    later_deltas = deltas_of(totals[:, :, :wide_size], low, later)
    earlier_deltas = deltas_of(second_totals, low, earlier)

    own_factors = None
    for (hidden, gate_delta, up_delta), columns in (
        (later_deltas, later),
        (earlier_deltas, earlier),
    ):
        term = jnp.concatenate(
            [
                matrix_multiply(hidden, down_adapter_first[columns]),
                multiply_right_transposed(gate_delta, gate_adapter_second[:, columns]),
                multiply_right_transposed(up_delta, up_adapter_second[:, columns]),
            ],
            axis=1,
        )
        own_factors = term if own_factors is None else own_factors + term

    def to_all(value, axis):
        count = lax.axis_size(axis)
        return lax.all_to_all(
            jnp.broadcast_to(value[None], (count,) + value.shape), axis, 0, 0, tiled=True
        )

    packed = jnp.concatenate(
        [
            piece
            for which, rank_part in ((1, low[0]), (2, low[1]), (0, low[2]))
            for piece in (earlier_deltas[which], later_deltas[which], rank_part)
        ],
        axis=1,
    )
    piece = lax.all_gather(packed, "col", axis=0, tiled=True)
    factor_parts = to_all(own_factors.astype(jnp.bfloat16), "row")
    own_factors = jnp.sum(factor_parts.astype(jnp.float32), axis=0).astype(jnp.bfloat16)
    factors = to_all(own_factors, "col").reshape(tokens_all, 3 * rank)
    piece, factors = lax.optimization_barrier((piece, factors))
    packed_width = hidden_units + rank
    piece_gate, piece_up, piece_hidden = [
        piece[:, i * packed_width : i * packed_width + hidden_units] for i in range(3)
    ]
    gate_low, up_low, down_low = [
        piece[:, i * packed_width + hidden_units : (i + 1) * packed_width] for i in range(3)
    ]

    def input_part(which):
        def term(deltas, weight):
            lines = deltas.reshape(chips, 2, share_tokens, hidden_units)
            chosen = lax.dynamic_index_in_dim(lines, which, 1, keepdims=False)
            return multiply_right_transposed(
                chosen.reshape(chips * share_tokens, hidden_units), weight
            )

        return term(piece_gate, frozen_gate_weight) + term(piece_up, frozen_up_weight)

    other = lax.ppermute(input_part(1 - core).astype(jnp.bfloat16), "row", swap)
    share = (input_part(core) + other.astype(jnp.float32)).astype(jnp.bfloat16)
    shares = lax.all_to_all(share, "row", 0, 0, axis_index_groups=same_core, tiled=True)
    summed = jnp.sum(shares.reshape(chips, share_tokens, width).astype(jnp.float32), axis=0)

    first_token = lax.axis_index("row") * share_tokens
    row_factors = lax.dynamic_slice_in_dim(factors, first_token, share_tokens, 0)
    activation_gradient = (
        summed
        + adapter_scale
        * (
            multiply_right_transposed(row_factors[:, rank : 2 * rank], gate_adapter_first)
            + multiply_right_transposed(row_factors[:, 2 * rank :], up_adapter_first)
        )
    ).astype(jnp.bfloat16)

    features = width // row_count
    first_feature = lax.axis_index("row") * features
    activation_columns = lax.dynamic_slice_in_dim(full_act, first_feature, features, 1)
    activation_columns = activation_columns.reshape(side, side, pair_tokens, features)
    activation_columns = activation_columns.swapaxes(0, 1).reshape(tokens_all, features)
    output_columns = lax.dynamic_slice_in_dim(full_out, first_feature, features, 1)
    first_gradients = adapter_scale * multiply_left_transposed(
        activation_columns, factors[:, rank:]
    )
    gate_adapter_first_gradient = first_gradients[:, :rank]
    up_adapter_first_gradient = first_gradients[:, rank:]
    down_adapter_second_gradient = adapter_scale * multiply_left_transposed(
        factors[:, :rank], output_columns
    )

    gate_adapter_second_gradient = adapter_scale * multiply_left_transposed(gate_low, piece_gate)
    up_adapter_second_gradient = adapter_scale * multiply_left_transposed(up_low, piece_up)
    down_adapter_first_gradient = adapter_scale * multiply_left_transposed(piece_hidden, down_low)
    return (
        activation_gradient,
        gate_adapter_first_gradient,
        gate_adapter_second_gradient,
        up_adapter_first_gradient,
        up_adapter_second_gradient,
        down_adapter_first_gradient,
        down_adapter_second_gradient,
    )


def solution(mesh):
    return jax.shard_map(
        body,
        mesh=mesh,
        in_specs=(
            P("row", "col"),
            P("row", "col"),
            P("col", "row"),
            P("col", "row"),
            P("row", "col"),
            P("col", None),
            P(None, "row"),
            P("col", None),
            P(None, "row"),
            P("row", None),
            P(None, "col"),
        ),
        out_specs=(
            P("row", "col"),
            P(("col", "row"), None),
            P(None, "row"),
            P(("col", "row"), None),
            P(None, "row"),
            P("row", None),
            P(None, ("col", "row")),
        ),
        check_vma=False,
    )
```

```python
import math

import jax
import jax.numpy as jnp
from jax import lax
from jax.sharding import PartitionSpec as P

adapter_scale = 0.5


def matrix_multiply(left, right):
    return jnp.dot(left, right, preferred_element_type=jnp.float32)


def multiply_right_transposed(left, right):
    return lax.dot_general(
        left, right, (((1,), (1,)), ((), ())), preferred_element_type=jnp.float32
    )


def multiply_left_transposed(left, right):
    return lax.dot_general(
        left, right, (((0,), (0,)), ((), ())), preferred_element_type=jnp.float32
    )


def pointwise(gate_activation, up_activation, backward_result):
    sigmoid_gate = jax.nn.sigmoid(gate_activation)
    silu_gate = gate_activation * sigmoid_gate
    hidden_state = (silu_gate * up_activation).astype(jnp.bfloat16)
    up_gradient_term = (backward_result * silu_gate).astype(jnp.bfloat16)
    gate_gradient_term = (
        backward_result
        * up_activation
        * sigmoid_gate
        * (1.0 + gate_activation * (1.0 - sigmoid_gate))
    ).astype(jnp.bfloat16)
    return (hidden_state, gate_gradient_term, up_gradient_term)


def shifted(size, step):
    return [(i, (i + step) % size) for i in range(size)]


def two_way_rings(axis, operands, up_steps, arrive):
    size = lax.axis_size(axis)
    state = list(operands)
    for step in range(1, size // 2 + 1):
        for stream, steps in enumerate(up_steps):
            up, down = state[stream]
            if step <= steps:
                up = lax.ppermute(up, axis, shifted(size, 1))
            if step <= size - 1 - steps:
                down = lax.ppermute(down, axis, shifted(size, -1))
            state[stream] = arrive(stream, step, up, down)
    return state


def ring_sums(block_ofs, axis, up_steps, operands):
    size = lax.axis_size(axis)
    here = lax.axis_index(axis)

    def block(stream, offset):
        return block_ofs[stream](lax.rem(here + offset + size, size))

    def arrive(stream, step, up, down):
        ups = up_steps[stream]
        downs = size - 1 - ups
        if step < ups:
            up = (up.astype(jnp.float32) + block(stream, ups - step)).astype(jnp.bfloat16)
        if step < downs:
            down = (down.astype(jnp.float32) + block(stream, step - downs)).astype(jnp.bfloat16)
        return up, down

    return [
        up.astype(jnp.float32) + down.astype(jnp.float32) + block(stream, 0)
        for stream, (up, down) in enumerate(two_way_rings(axis, operands, up_steps, arrive))
    ]


def gather_tokens(activations, output_gradient):
    tokens, width = activations.shape
    row_count = lax.axis_size("row")
    side = math.isqrt(row_count // 2)
    here = lax.axis_index("row")
    core = lax.rem(here, 2)
    x = here // (2 * side)
    y = lax.rem(here // 2, side)
    first_at = jnp.where(core == 0, x, y)
    second_at = jnp.where(core == 0, y, x)

    def moves(first, second):
        pairs = []
        for source in range(row_count):
            sx, sy, sc = source // (2 * side), source // 2 % side, source % 2
            step_x, step_y = (first, second) if sc == 0 else (second, first)
            pairs.append(
                (source, (((sx + step_x) % side) * side + (sy + step_y) % side) * 2 + sc)
            )
        return pairs

    swap = [(source, source ^ 1) for source in range(row_count)]

    def to_other_core(value):
        return lax.ppermute(value, "row", swap)

    mine = jnp.where(core == 0, activations, output_gradient)
    given = to_other_core(jnp.where(core == 0, output_gradient, activations))
    pair = jnp.concatenate(
        [jnp.where(core == 0, mine, given), jnp.where(core == 0, given, mine)], axis=0
    )
    slab = jnp.zeros((side,) + pair.shape, pair.dtype)
    slab = lax.dynamic_update_index_in_dim(slab, pair, first_at, 0)
    for step in (1, -1, 2):
        got = lax.ppermute(pair, "row", moves(step, 0))
        slab = lax.dynamic_update_index_in_dim(
            slab, got, lax.rem(first_at - step + side, side), 0
        )
    slab = slab.reshape(side * 2 * tokens, width)
    half = slab.shape[0] // 2

    before = lax.ppermute(slab, "row", moves(0, 1))
    after = lax.ppermute(slab, "row", moves(0, -1))
    far = jnp.concatenate(
        [
            lax.ppermute(slab[:half], "row", moves(0, 2)),
            lax.ppermute(slab[half:], "row", moves(0, -2)),
        ],
        axis=0,
    )
    gathered = jnp.zeros((2, side) + slab.shape, slab.dtype)
    for offset, part in ((0, slab), (-1, before), (1, after), (2, far)):
        for which, value, at in (
            (core, part, second_at),
            (1 - core, to_other_core(part), first_at),
        ):
            gathered = lax.dynamic_update_slice(
                gathered, value[None, None], (which, lax.rem(at + offset + side, side), 0, 0)
            )
    shape = (side, side, 2 * tokens, width)
    return gathered[0].reshape(shape), gathered[1].reshape(shape)


def body(
    activations,
    output_gradient,
    frozen_gate_weight,
    frozen_up_weight,
    frozen_down_weight,
    gate_adapter_first,
    gate_adapter_second,
    up_adapter_first,
    up_adapter_second,
    down_adapter_first,
    down_leave,
):
    share_tokens, width = activations.shape
    rank, hidden_units = gate_adapter_second.shape
    row_count = lax.axis_size("row")
    col_count = lax.axis_size("col")
    tokens_all = share_tokens * row_count
    col_tokens = tokens_all // col_count
    chips = row_count // 2
    core = lax.rem(lax.axis_index("row"), 2)
    cut = (hidden_units - rank) // 2
    wide_size = hidden_units - cut
    swap = [(i, i ^ 1) for i in range(row_count)]
    same_core = [[2 * chip + c for chip in range(chips)] for c in range(2)]

    gathered_act, gathered_out = gather_tokens(activations, output_gradient)
    side = gathered_act.shape[0]
    pair_tokens = 2 * share_tokens
    pairs_per_col = col_tokens // pair_tokens
    blocks_per_line = side // pairs_per_col
    full_act = gathered_act.reshape(tokens_all, width)
    full_out = gathered_out.reshape(tokens_all, width)

    def blocks_of(first, size):
        def lines_block(partial, index):
            lines = partial.reshape(side, side, pair_tokens, -1)
            place = (lax.rem(index, blocks_per_line) * pairs_per_col, index // blocks_per_line)
            chosen = lax.dynamic_slice(
                lines, place + (0, first), (pairs_per_col, 1, pair_tokens, size)
            )
            return chosen.reshape(col_tokens, size)

        def block_of(index):
            return jnp.stack(
                [
                    lines_block(partials[0], index),
                    lines_block(partials[1], index),
                    lax.dynamic_slice(
                        partials[2], (index * col_tokens, first), (col_tokens, size)
                    ),
                ]
            )

        return block_of

    def first_operands(block_of, ups):
        here = lax.axis_index("col")
        return tuple(
            block_of(lax.rem(here + offset + col_count, col_count)).astype(jnp.bfloat16)
            for offset in (ups, ups + 1 - col_count)
        )

    def deltas_of(totals, low, columns):
        gate_activation = totals[0] + adapter_scale * matrix_multiply(
            low[0], gate_adapter_second[:, columns]
        )
        up_activation = totals[1] + adapter_scale * matrix_multiply(
            low[1], up_adapter_second[:, columns]
        )
        backward_result = totals[2] + adapter_scale * multiply_right_transposed(
            low[2], down_adapter_first[columns]
        )
        return pointwise(gate_activation, up_activation, backward_result)

    partials = lax.optimization_barrier(
        (
            multiply_right_transposed(
                full_act, jnp.concatenate([frozen_gate_weight, gate_adapter_first], axis=1).T
            ),
            multiply_right_transposed(
                full_act, jnp.concatenate([frozen_up_weight, up_adapter_first], axis=1).T
            ),
            multiply_right_transposed(
                full_out, jnp.concatenate([frozen_down_weight, down_leave], axis=0)
            ),
        )
    )
    later = slice(cut, hidden_units)
    earlier = slice(0, cut)
    up_steps = (col_count // 2, col_count - 1 - col_count // 2)
    block_ofs = (blocks_of(cut, wide_size + rank), blocks_of(0, cut))
    totals, second_totals = ring_sums(
        block_ofs,
        "col",
        up_steps,
        [first_operands(block_of, ups) for block_of, ups in zip(block_ofs, up_steps)],
    )
    low = totals[:, :, wide_size:].astype(jnp.bfloat16)
    later_deltas = deltas_of(totals[:, :, :wide_size], low, later)
    earlier_deltas = deltas_of(second_totals, low, earlier)

    packed = jnp.concatenate(
        [
            piece
            for which, rank_part in ((1, low[0]), (2, low[1]), (0, low[2]))
            for piece in (earlier_deltas[which], later_deltas[which], rank_part)
        ],
        axis=1,
    )
    piece = lax.all_gather(packed, "col", axis=0, tiled=True)
    packed_width = hidden_units + rank

    def packed_part(which):
        return packed[:, which * packed_width : which * packed_width + hidden_units]

    own_factors = jnp.concatenate(
        [
            matrix_multiply(packed_part(2), down_adapter_first),
            multiply_right_transposed(packed_part(0), gate_adapter_second),
            multiply_right_transposed(packed_part(1), up_adapter_second),
        ],
        axis=1,
    ).astype(jnp.bfloat16)

    def to_all(value, axis, count, groups=None):
        copies = jnp.broadcast_to(value[None], (count,) + value.shape)
        return lax.all_to_all(copies, axis, 0, 0, axis_index_groups=groups, tiled=True)

    other_factors = lax.ppermute(own_factors, "row", swap)
    own_factors = own_factors.astype(jnp.float32) + other_factors.astype(jnp.float32)
    factor_parts = to_all(own_factors.astype(jnp.bfloat16), "row", chips, same_core)
    own_factors = jnp.sum(factor_parts.astype(jnp.float32), axis=0).astype(jnp.bfloat16)
    factors = to_all(own_factors, "col", col_count).reshape(tokens_all, 3 * rank)
    piece, factors = lax.optimization_barrier((piece, factors))
    piece_gate, piece_up, piece_hidden = [
        piece[:, i * packed_width : i * packed_width + hidden_units] for i in range(3)
    ]
    gate_low, up_low, down_low = [
        piece[:, i * packed_width + hidden_units : (i + 1) * packed_width] for i in range(3)
    ]

    def input_part(which):
        def term(deltas, weight):
            lines = deltas.reshape(chips, 2, share_tokens, hidden_units)
            chosen = lax.dynamic_index_in_dim(lines, which, 1, keepdims=False)
            return multiply_right_transposed(
                chosen.reshape(chips * share_tokens, hidden_units), weight
            )

        return term(piece_gate, frozen_gate_weight) + term(piece_up, frozen_up_weight)

    other = lax.ppermute(input_part(1 - core).astype(jnp.bfloat16), "row", swap)
    share = (input_part(core) + other.astype(jnp.float32)).astype(jnp.bfloat16)
    factors, share = lax.optimization_barrier((factors, share))
    shares = lax.all_to_all(share, "row", 0, 0, axis_index_groups=same_core, tiled=True)
    summed = jnp.sum(shares.reshape(chips, share_tokens, width).astype(jnp.float32), axis=0)

    first_token = lax.axis_index("row") * share_tokens
    row_factors = lax.dynamic_slice_in_dim(factors, first_token, share_tokens, 0)
    activation_gradient = (
        summed
        + adapter_scale
        * (
            multiply_right_transposed(row_factors[:, rank : 2 * rank], gate_adapter_first)
            + multiply_right_transposed(row_factors[:, 2 * rank :], up_adapter_first)
        )
    ).astype(jnp.bfloat16)

    features = width // row_count
    first_feature = lax.axis_index("row") * features
    activation_columns = lax.dynamic_slice_in_dim(full_act, first_feature, features, 1)
    activation_columns = activation_columns.reshape(side, side, pair_tokens, features)
    activation_columns = activation_columns.swapaxes(0, 1).reshape(tokens_all, features)
    output_columns = lax.dynamic_slice_in_dim(full_out, first_feature, features, 1)
    first_gradients = adapter_scale * multiply_left_transposed(
        activation_columns, factors[:, rank:]
    )
    gate_adapter_first_gradient = first_gradients[:, :rank]
    up_adapter_first_gradient = first_gradients[:, rank:]
    down_adapter_second_gradient = adapter_scale * multiply_left_transposed(
        factors[:, :rank], output_columns
    )

    gate_adapter_second_gradient = adapter_scale * multiply_left_transposed(gate_low, piece_gate)
    up_adapter_second_gradient = adapter_scale * multiply_left_transposed(up_low, piece_up)
    down_adapter_first_gradient = adapter_scale * multiply_left_transposed(piece_hidden, down_low)
    return (
        activation_gradient,
        gate_adapter_first_gradient,
        gate_adapter_second_gradient,
        up_adapter_first_gradient,
        up_adapter_second_gradient,
        down_adapter_first_gradient,
        down_adapter_second_gradient,
    )


def solution(mesh):
    return jax.shard_map(
        body,
        mesh=mesh,
        in_specs=(
            P("row", "col"),
            P("row", "col"),
            P("col", "row"),
            P("col", "row"),
            P("row", "col"),
            P("col", None),
            P(None, "row"),
            P("col", None),
            P(None, "row"),
            P("row", None),
            P(None, "col"),
        ),
        out_specs=(
            P("row", "col"),
            P(("col", "row"), None),
            P(None, "row"),
            P(("col", "row"), None),
            P(None, "row"),
            P("row", None),
            P(None, ("col", "row")),
        ),
        check_vma=False,
    )
```

```python
import math

import jax
import jax.numpy as jnp
from jax import lax
from jax.sharding import PartitionSpec as P

adapter_scale = 0.5


def matrix_multiply(left, right):
    return jnp.dot(left, right, preferred_element_type=jnp.float32)


def multiply_right_transposed(left, right):
    return lax.dot_general(
        left, right, (((1,), (1,)), ((), ())), preferred_element_type=jnp.float32
    )


def multiply_left_transposed(left, right):
    return lax.dot_general(
        left, right, (((0,), (0,)), ((), ())), preferred_element_type=jnp.float32
    )


def pointwise(gate_activation, up_activation, backward_result):
    sigmoid_gate = jax.nn.sigmoid(gate_activation)
    silu_gate = gate_activation * sigmoid_gate
    hidden_state = (silu_gate * up_activation).astype(jnp.bfloat16)
    up_gradient_term = (backward_result * silu_gate).astype(jnp.bfloat16)
    gate_gradient_term = (
        backward_result
        * up_activation
        * sigmoid_gate
        * (1.0 + gate_activation * (1.0 - sigmoid_gate))
    ).astype(jnp.bfloat16)
    return (hidden_state, gate_gradient_term, up_gradient_term)


def shifted(size, step):
    return [(i, (i + step) % size) for i in range(size)]


def ring_sums(block_ofs, axis, ways):
    size = lax.axis_size(axis)
    here = lax.axis_index(axis)
    far = size // 2

    def block(stream, offset):
        return block_ofs[stream](lax.rem(here + offset * ways[stream] + size, size))

    def send(stream, value, step):
        return lax.ppermute(
            value.astype(jnp.bfloat16), axis, shifted(size, step * ways[stream])
        ).astype(jnp.float32)

    streams = range(len(ways))
    ahead = []
    behind = []
    for stream in streams:
        ahead.append(
            send(stream, block(stream, far), 2) + send(stream, block(stream, far - 1), 1)
        )
        behind.append(send(stream, block(stream, 1 - far), -1))
    for offset in range(far - 2, 0, -1):
        for stream in streams:
            ahead[stream] = send(stream, ahead[stream] + block(stream, offset), 1)
            behind[stream] = send(stream, behind[stream] + block(stream, -offset), -1)
    return [ahead[stream] + behind[stream] + block(stream, 0) for stream in streams]


def gather_tokens(activations, output_gradient):
    tokens, width = activations.shape
    row_count = lax.axis_size("row")
    side = math.isqrt(row_count // 2)
    here = lax.axis_index("row")
    core = lax.rem(here, 2)
    x = here // (2 * side)
    y = lax.rem(here // 2, side)
    first_at = jnp.where(core == 0, x, y)
    second_at = jnp.where(core == 0, y, x)

    def moves(first, second):
        pairs = []
        for source in range(row_count):
            sx, sy, sc = source // (2 * side), source // 2 % side, source % 2
            step_x, step_y = (first, second) if sc == 0 else (second, first)
            pairs.append(
                (source, (((sx + step_x) % side) * side + (sy + step_y) % side) * 2 + sc)
            )
        return pairs

    swap = [(source, source ^ 1) for source in range(row_count)]

    def to_other_core(value):
        return lax.ppermute(value, "row", swap)

    mine = jnp.where(core == 0, activations, output_gradient)
    given = to_other_core(jnp.where(core == 0, output_gradient, activations))
    pair = jnp.concatenate(
        [jnp.where(core == 0, mine, given), jnp.where(core == 0, given, mine)], axis=0
    )
    slab = jnp.zeros((side,) + pair.shape, pair.dtype)
    slab = lax.dynamic_update_index_in_dim(slab, pair, first_at, 0)
    for step in (1, -1, 2):
        got = lax.ppermute(pair, "row", moves(step, 0))
        slab = lax.dynamic_update_index_in_dim(
            slab, got, lax.rem(first_at - step + side, side), 0
        )
    slab = slab.reshape(side * 2 * tokens, width)
    half = slab.shape[0] // 2

    before = lax.ppermute(slab, "row", moves(0, 1))
    after = lax.ppermute(slab, "row", moves(0, -1))
    far = jnp.concatenate(
        [
            lax.ppermute(slab[:half], "row", moves(0, 2)),
            lax.ppermute(slab[half:], "row", moves(0, -2)),
        ],
        axis=0,
    )
    gathered = jnp.zeros((2, side) + slab.shape, slab.dtype)
    for offset, part in ((0, slab), (-1, before), (1, after), (2, far)):
        for which, value, at in (
            (core, part, second_at),
            (1 - core, to_other_core(part), first_at),
        ):
            gathered = lax.dynamic_update_slice(
                gathered, value[None, None], (which, lax.rem(at + offset + side, side), 0, 0)
            )
    shape = (side, side, 2 * tokens, width)
    return gathered[0].reshape(shape), gathered[1].reshape(shape)


def body(
    activations,
    output_gradient,
    frozen_gate_weight,
    frozen_up_weight,
    frozen_down_weight,
    gate_adapter_first,
    gate_adapter_second,
    up_adapter_first,
    up_adapter_second,
    down_adapter_first,
    down_leave,
):
    share_tokens, width = activations.shape
    rank, hidden_units = gate_adapter_second.shape
    row_count = lax.axis_size("row")
    col_count = lax.axis_size("col")
    tokens_all = share_tokens * row_count
    col_tokens = tokens_all // col_count
    chips = row_count // 2
    core = lax.rem(lax.axis_index("row"), 2)
    cut = (hidden_units - rank) // 2
    wide_size = hidden_units - cut
    swap = [(i, i ^ 1) for i in range(row_count)]
    same_core = [[2 * chip + c for chip in range(chips)] for c in range(2)]

    gathered_act, gathered_out = gather_tokens(activations, output_gradient)
    side = gathered_act.shape[0]
    pair_tokens = 2 * share_tokens
    pairs_per_col = col_tokens // pair_tokens
    blocks_per_line = side // pairs_per_col
    full_act = gathered_act.reshape(tokens_all, width)
    full_out = gathered_out.reshape(tokens_all, width)

    def blocks_of(first, size):
        def lines_block(partial, index):
            lines = partial.reshape(side, side, pair_tokens, -1)
            place = (lax.rem(index, blocks_per_line) * pairs_per_col, index // blocks_per_line)
            chosen = lax.dynamic_slice(
                lines, place + (0, first), (pairs_per_col, 1, pair_tokens, size)
            )
            return chosen.reshape(col_tokens, size)

        def block_of(index):
            return jnp.stack(
                [
                    lines_block(partials[0], index),
                    lines_block(partials[1], index),
                    lax.dynamic_slice(
                        partials[2], (index * col_tokens, first), (col_tokens, size)
                    ),
                ]
            )

        return block_of

    def deltas_of(totals, low, columns):
        gate_activation = totals[0] + adapter_scale * matrix_multiply(
            low[0], gate_adapter_second[:, columns]
        )
        up_activation = totals[1] + adapter_scale * matrix_multiply(
            low[1], up_adapter_second[:, columns]
        )
        backward_result = totals[2] + adapter_scale * multiply_right_transposed(
            low[2], down_adapter_first[columns]
        )
        return pointwise(gate_activation, up_activation, backward_result)

    partials = lax.optimization_barrier(
        (
            multiply_right_transposed(
                full_act, jnp.concatenate([frozen_gate_weight, gate_adapter_first], axis=1).T
            ),
            multiply_right_transposed(
                full_act, jnp.concatenate([frozen_up_weight, up_adapter_first], axis=1).T
            ),
            multiply_right_transposed(
                full_out, jnp.concatenate([frozen_down_weight, down_leave], axis=0)
            ),
        )
    )
    later = slice(cut, hidden_units)
    earlier = slice(0, cut)
    totals, second_totals = ring_sums(
        (blocks_of(cut, wide_size + rank), blocks_of(0, cut)), "col", (1, -1)
    )
    low = totals[:, :, wide_size:].astype(jnp.bfloat16)
    later_deltas = deltas_of(totals[:, :, :wide_size], low, later)
    earlier_deltas = deltas_of(second_totals, low, earlier)

    packed = jnp.concatenate(
        [
            piece
            for which, rank_part in ((1, low[0]), (2, low[1]), (0, low[2]))
            for piece in (earlier_deltas[which], later_deltas[which], rank_part)
        ],
        axis=1,
    )
    piece = lax.all_gather(packed, "col", axis=0, tiled=True)
    packed_width = hidden_units + rank

    def packed_part(which):
        return packed[:, which * packed_width : which * packed_width + hidden_units]

    own_factors = jnp.concatenate(
        [
            matrix_multiply(packed_part(2), down_adapter_first),
            multiply_right_transposed(packed_part(0), gate_adapter_second),
            multiply_right_transposed(packed_part(1), up_adapter_second),
        ],
        axis=1,
    ).astype(jnp.bfloat16)

    def to_all(value, axis, count, groups=None):
        copies = jnp.broadcast_to(value[None], (count,) + value.shape)
        return lax.all_to_all(copies, axis, 0, 0, axis_index_groups=groups, tiled=True)

    other_factors = lax.ppermute(own_factors, "row", swap)
    own_factors = own_factors.astype(jnp.float32) + other_factors.astype(jnp.float32)
    factor_parts = to_all(own_factors.astype(jnp.bfloat16), "row", chips, same_core)
    own_factors = jnp.sum(factor_parts.astype(jnp.float32), axis=0).astype(jnp.bfloat16)
    factors = to_all(own_factors, "col", col_count).reshape(tokens_all, 3 * rank)
    piece, factors = lax.optimization_barrier((piece, factors))
    piece_gate, piece_up, piece_hidden = [
        piece[:, i * packed_width : i * packed_width + hidden_units] for i in range(3)
    ]
    gate_low, up_low, down_low = [
        piece[:, i * packed_width + hidden_units : (i + 1) * packed_width] for i in range(3)
    ]

    def input_part(which):
        def term(deltas, weight):
            lines = deltas.reshape(chips, 2, share_tokens, hidden_units)
            chosen = lax.dynamic_index_in_dim(lines, which, 1, keepdims=False)
            return multiply_right_transposed(
                chosen.reshape(chips * share_tokens, hidden_units), weight
            )

        return term(piece_gate, frozen_gate_weight) + term(piece_up, frozen_up_weight)

    other = lax.ppermute(input_part(1 - core).astype(jnp.bfloat16), "row", swap)
    share = (input_part(core) + other.astype(jnp.float32)).astype(jnp.bfloat16)
    shares = lax.all_to_all(share, "row", 0, 0, axis_index_groups=same_core, tiled=True)
    summed = jnp.sum(shares.reshape(chips, share_tokens, width).astype(jnp.float32), axis=0)

    first_token = lax.axis_index("row") * share_tokens
    row_factors = lax.dynamic_slice_in_dim(factors, first_token, share_tokens, 0)
    activation_gradient = (
        summed
        + adapter_scale
        * (
            multiply_right_transposed(row_factors[:, rank : 2 * rank], gate_adapter_first)
            + multiply_right_transposed(row_factors[:, 2 * rank :], up_adapter_first)
        )
    ).astype(jnp.bfloat16)

    features = width // row_count
    first_feature = lax.axis_index("row") * features
    activation_columns = lax.dynamic_slice_in_dim(full_act, first_feature, features, 1)
    activation_columns = activation_columns.reshape(side, side, pair_tokens, features)
    activation_columns = activation_columns.swapaxes(0, 1).reshape(tokens_all, features)
    output_columns = lax.dynamic_slice_in_dim(full_out, first_feature, features, 1)
    first_gradients = adapter_scale * multiply_left_transposed(
        activation_columns, factors[:, rank:]
    )
    gate_adapter_first_gradient = first_gradients[:, :rank]
    up_adapter_first_gradient = first_gradients[:, rank:]
    down_adapter_second_gradient = adapter_scale * multiply_left_transposed(
        factors[:, :rank], output_columns
    )

    gate_adapter_second_gradient = adapter_scale * multiply_left_transposed(gate_low, piece_gate)
    up_adapter_second_gradient = adapter_scale * multiply_left_transposed(up_low, piece_up)
    down_adapter_first_gradient = adapter_scale * multiply_left_transposed(piece_hidden, down_low)
    return (
        activation_gradient,
        gate_adapter_first_gradient,
        gate_adapter_second_gradient,
        up_adapter_first_gradient,
        up_adapter_second_gradient,
        down_adapter_first_gradient,
        down_adapter_second_gradient,
    )


def solution(mesh):
    return jax.shard_map(
        body,
        mesh=mesh,
        in_specs=(
            P("row", "col"),
            P("row", "col"),
            P("col", "row"),
            P("col", "row"),
            P("row", "col"),
            P("col", None),
            P(None, "row"),
            P("col", None),
            P(None, "row"),
            P("row", None),
            P(None, "col"),
        ),
        out_specs=(
            P("row", "col"),
            P(("col", "row"), None),
            P(None, "row"),
            P(("col", "row"), None),
            P(None, "row"),
            P("row", None),
            P(None, ("col", "row")),
        ),
        check_vma=False,
    )
```

```python
import math

import jax
import jax.numpy as jnp
from jax import lax
from jax.sharding import PartitionSpec as P

adapter_scale = 0.5


def matrix_multiply(left, right):
    return jnp.dot(left, right, preferred_element_type=jnp.float32)


def multiply_right_transposed(left, right):
    return lax.dot_general(
        left, right, (((1,), (1,)), ((), ())), preferred_element_type=jnp.float32
    )


def multiply_left_transposed(left, right):
    return lax.dot_general(
        left, right, (((0,), (0,)), ((), ())), preferred_element_type=jnp.float32
    )


def pointwise(gate_activation, up_activation, backward_result):
    sigmoid_gate = jax.nn.sigmoid(gate_activation)
    silu_gate = gate_activation * sigmoid_gate
    hidden_state = (silu_gate * up_activation).astype(jnp.bfloat16)
    up_gradient_term = (backward_result * silu_gate).astype(jnp.bfloat16)
    gate_gradient_term = (
        backward_result
        * up_activation
        * sigmoid_gate
        * (1.0 + gate_activation * (1.0 - sigmoid_gate))
    ).astype(jnp.bfloat16)
    return (hidden_state, gate_gradient_term, up_gradient_term)


def shifted(size, step):
    return [(i, (i + step) % size) for i in range(size)]


def ring_sums(block_ofs, axis, ways):
    size = lax.axis_size(axis)
    here = lax.axis_index(axis)
    far = size // 2

    def block(stream, offset):
        return block_ofs[stream](lax.rem(here + offset * ways[stream] + size, size))

    def send(stream, value, step):
        return lax.ppermute(
            value.astype(jnp.bfloat16), axis, shifted(size, step * ways[stream])
        ).astype(jnp.float32)

    streams = range(len(ways))
    ahead = []
    behind = []
    for stream in streams:
        ahead.append(
            send(stream, block(stream, far), 2) + send(stream, block(stream, far - 1), 1)
        )
        behind.append(send(stream, block(stream, 1 - far), -1))
    for offset in range(far - 2, 0, -1):
        for stream in streams:
            ahead[stream] = send(stream, ahead[stream] + block(stream, offset), 1)
            behind[stream] = send(stream, behind[stream] + block(stream, -offset), -1)
    return [ahead[stream] + behind[stream] + block(stream, 0) for stream in streams]


def gather_tokens(activations, output_gradient, use):
    tokens, width = activations.shape
    row_count = lax.axis_size("row")
    side = math.isqrt(row_count // 2)
    here = lax.axis_index("row")
    core = lax.rem(here, 2)
    x = here // (2 * side)
    y = lax.rem(here // 2, side)
    first_at = jnp.where(core == 0, x, y)
    second_at = jnp.where(core == 0, y, x)

    def moves(first, second):
        pairs = []
        for source in range(row_count):
            sx, sy, sc = source // (2 * side), source // 2 % side, source % 2
            step_x, step_y = (first, second) if sc == 0 else (second, first)
            pairs.append(
                (source, (((sx + step_x) % side) * side + (sy + step_y) % side) * 2 + sc)
            )
        return pairs

    swap = [(source, source ^ 1) for source in range(row_count)]

    def to_other_core(value):
        return lax.ppermute(value, "row", swap)

    mine = jnp.where(core == 0, activations, output_gradient)
    given = to_other_core(jnp.where(core == 0, output_gradient, activations))
    pair = jnp.concatenate(
        [jnp.where(core == 0, mine, given), jnp.where(core == 0, given, mine)], axis=0
    )
    slab = jnp.zeros((side,) + pair.shape, pair.dtype)
    slab = lax.dynamic_update_index_in_dim(slab, pair, first_at, 0)
    for step in (1, -1, 2):
        got = lax.ppermute(pair, "row", moves(step, 0))
        slab = lax.dynamic_update_index_in_dim(
            slab, got, lax.rem(first_at - step + side, side), 0
        )
    slab = slab.reshape(side * 2 * tokens, width)
    half = slab.shape[0] // 2

    before = lax.ppermute(slab, "row", moves(0, 1))
    after = lax.ppermute(slab, "row", moves(0, -1))
    far = (
        lax.ppermute(slab[:half], "row", moves(0, 2)),
        lax.ppermute(slab[half:], "row", moves(0, -2)),
    )
    used = ()
    for offset, part in ((0, slab), (-1, before), (1, after), (2, far)):
        if part is far:
            part = jnp.concatenate(lax.optimization_barrier(far + used)[:2], axis=0)
        given = to_other_core(part)
        used = use(
            jnp.where(core == 0, part, given),
            lax.rem(y + offset + side, side),
            jnp.where(core == 0, given, part),
            lax.rem(x + offset + side, side),
        )


def body(
    activations,
    output_gradient,
    frozen_gate_weight,
    frozen_up_weight,
    frozen_down_weight,
    gate_adapter_first,
    gate_adapter_second,
    up_adapter_first,
    up_adapter_second,
    down_adapter_first,
    down_leave,
):
    share_tokens, width = activations.shape
    rank, hidden_units = gate_adapter_second.shape
    row_count = lax.axis_size("row")
    col_count = lax.axis_size("col")
    tokens_all = share_tokens * row_count
    col_tokens = tokens_all // col_count
    chips = row_count // 2
    core = lax.rem(lax.axis_index("row"), 2)
    cut = (hidden_units - rank) // 2
    wide_size = hidden_units - cut
    swap = [(i, i ^ 1) for i in range(row_count)]
    same_core = [[2 * chip + c for chip in range(chips)] for c in range(2)]

    side = math.isqrt(chips)
    pair_tokens = 2 * share_tokens
    pairs_per_col = col_tokens // pair_tokens
    blocks_per_line = side // pairs_per_col
    features = width // row_count
    first_feature = lax.axis_index("row") * features

    weights = (
        jnp.concatenate([frozen_gate_weight, gate_adapter_first], axis=1).T,
        jnp.concatenate([frozen_up_weight, up_adapter_first], axis=1).T,
        jnp.concatenate([frozen_down_weight, down_leave], axis=0),
    )
    slab_tokens = side * pair_tokens
    partials = [
        jnp.zeros((side, slab_tokens, hidden_units + rank), jnp.float32) for _ in weights
    ]
    columns_kept = [jnp.zeros((side, slab_tokens, features), jnp.bfloat16) for _ in range(2)]

    def use_slabs(act_slab, act_at, out_slab, out_at):
        for i, (part, at) in enumerate(
            ((act_slab, act_at), (act_slab, act_at), (out_slab, out_at))
        ):
            partials[i] = lax.dynamic_update_index_in_dim(
                partials[i], multiply_right_transposed(part, weights[i]), at, 0
            )
        for i, (part, at) in enumerate(((act_slab, act_at), (out_slab, out_at))):
            kept = lax.dynamic_slice_in_dim(part, first_feature, features, 1)
            columns_kept[i] = lax.dynamic_update_index_in_dim(columns_kept[i], kept, at, 0)
        return tuple(partials)

    gather_tokens(activations, output_gradient, use_slabs)
    partials = lax.optimization_barrier(
        tuple(partial.reshape(tokens_all, hidden_units + rank) for partial in partials)
    )

    def blocks_of(first, size):
        def lines_block(partial, index):
            lines = partial.reshape(side, side, pair_tokens, -1)
            place = (lax.rem(index, blocks_per_line) * pairs_per_col, index // blocks_per_line)
            chosen = lax.dynamic_slice(
                lines, place + (0, first), (pairs_per_col, 1, pair_tokens, size)
            )
            return chosen.reshape(col_tokens, size)

        def block_of(index):
            return jnp.stack(
                [
                    lines_block(partials[0], index),
                    lines_block(partials[1], index),
                    lax.dynamic_slice(
                        partials[2], (index * col_tokens, first), (col_tokens, size)
                    ),
                ]
            )

        return block_of

    def deltas_of(totals, low, columns):
        gate_activation = totals[0] + adapter_scale * matrix_multiply(
            low[0], gate_adapter_second[:, columns]
        )
        up_activation = totals[1] + adapter_scale * matrix_multiply(
            low[1], up_adapter_second[:, columns]
        )
        backward_result = totals[2] + adapter_scale * multiply_right_transposed(
            low[2], down_adapter_first[columns]
        )
        return pointwise(gate_activation, up_activation, backward_result)

    later = slice(cut, hidden_units)
    earlier = slice(0, cut)
    totals, second_totals = ring_sums(
        (blocks_of(cut, wide_size + rank), blocks_of(0, cut)), "col", (1, -1)
    )
    low = totals[:, :, wide_size:].astype(jnp.bfloat16)
    later_deltas = deltas_of(totals[:, :, :wide_size], low, later)
    earlier_deltas = deltas_of(second_totals, low, earlier)

    packed = jnp.concatenate(
        [
            piece
            for which, rank_part in ((1, low[0]), (2, low[1]), (0, low[2]))
            for piece in (earlier_deltas[which], later_deltas[which], rank_part)
        ],
        axis=1,
    )
    piece = lax.all_gather(packed, "col", axis=0, tiled=True)
    packed_width = hidden_units + rank

    def packed_part(which):
        return packed[:, which * packed_width : which * packed_width + hidden_units]

    own_factors = jnp.concatenate(
        [
            matrix_multiply(packed_part(2), down_adapter_first),
            multiply_right_transposed(packed_part(0), gate_adapter_second),
            multiply_right_transposed(packed_part(1), up_adapter_second),
        ],
        axis=1,
    ).astype(jnp.bfloat16)

    def to_all(value, axis, count, groups=None):
        copies = jnp.broadcast_to(value[None], (count,) + value.shape)
        return lax.all_to_all(copies, axis, 0, 0, axis_index_groups=groups, tiled=True)

    other_factors = lax.ppermute(own_factors, "row", swap)
    own_factors = own_factors.astype(jnp.float32) + other_factors.astype(jnp.float32)
    factor_parts = to_all(own_factors.astype(jnp.bfloat16), "row", chips, same_core)
    own_factors = jnp.sum(factor_parts.astype(jnp.float32), axis=0).astype(jnp.bfloat16)
    factors = to_all(own_factors, "col", col_count).reshape(tokens_all, 3 * rank)
    piece, factors = lax.optimization_barrier((piece, factors))
    piece_gate, piece_up, piece_hidden = [
        piece[:, i * packed_width : i * packed_width + hidden_units] for i in range(3)
    ]
    gate_low, up_low, down_low = [
        piece[:, i * packed_width + hidden_units : (i + 1) * packed_width] for i in range(3)
    ]

    def input_part(which):
        def term(deltas, weight):
            lines = deltas.reshape(chips, 2, share_tokens, hidden_units)
            chosen = lax.dynamic_index_in_dim(lines, which, 1, keepdims=False)
            return multiply_right_transposed(
                chosen.reshape(chips * share_tokens, hidden_units), weight
            )

        return term(piece_gate, frozen_gate_weight) + term(piece_up, frozen_up_weight)

    other = lax.ppermute(input_part(1 - core).astype(jnp.bfloat16), "row", swap)
    share = (input_part(core) + other.astype(jnp.float32)).astype(jnp.bfloat16)
    shares = lax.all_to_all(share, "row", 0, 0, axis_index_groups=same_core, tiled=True)
    summed = jnp.sum(shares.reshape(chips, share_tokens, width).astype(jnp.float32), axis=0)

    first_token = lax.axis_index("row") * share_tokens
    row_factors = lax.dynamic_slice_in_dim(factors, first_token, share_tokens, 0)
    activation_gradient = (
        summed
        + adapter_scale
        * (
            multiply_right_transposed(row_factors[:, rank : 2 * rank], gate_adapter_first)
            + multiply_right_transposed(row_factors[:, 2 * rank :], up_adapter_first)
        )
    ).astype(jnp.bfloat16)

    activation_columns = columns_kept[0].reshape(side, side, pair_tokens, features)
    activation_columns = activation_columns.swapaxes(0, 1).reshape(tokens_all, features)
    output_columns = columns_kept[1].reshape(tokens_all, features)
    first_gradients = adapter_scale * multiply_left_transposed(
        activation_columns, factors[:, rank:]
    )
    gate_adapter_first_gradient = first_gradients[:, :rank]
    up_adapter_first_gradient = first_gradients[:, rank:]
    down_adapter_second_gradient = adapter_scale * multiply_left_transposed(
        factors[:, :rank], output_columns
    )

    gate_adapter_second_gradient = adapter_scale * multiply_left_transposed(gate_low, piece_gate)
    up_adapter_second_gradient = adapter_scale * multiply_left_transposed(up_low, piece_up)
    down_adapter_first_gradient = adapter_scale * multiply_left_transposed(piece_hidden, down_low)
    return (
        activation_gradient,
        gate_adapter_first_gradient,
        gate_adapter_second_gradient,
        up_adapter_first_gradient,
        up_adapter_second_gradient,
        down_adapter_first_gradient,
        down_adapter_second_gradient,
    )


def solution(mesh):
    return jax.shard_map(
        body,
        mesh=mesh,
        in_specs=(
            P("row", "col"),
            P("row", "col"),
            P("col", "row"),
            P("col", "row"),
            P("row", "col"),
            P("col", None),
            P(None, "row"),
            P("col", None),
            P(None, "row"),
            P("row", None),
            P(None, "col"),
        ),
        out_specs=(
            P("row", "col"),
            P(("col", "row"), None),
            P(None, "row"),
            P(("col", "row"), None),
            P(None, "row"),
            P("row", None),
            P(None, ("col", "row")),
        ),
        check_vma=False,
    )
```

```python
import math

import jax
import jax.numpy as jnp
from jax import lax
from jax.sharding import PartitionSpec as P

adapter_scale = 0.5


def matrix_multiply(left, right):
    return jnp.dot(left, right, preferred_element_type=jnp.float32)


def multiply_right_transposed(left, right):
    return lax.dot_general(
        left, right, (((1,), (1,)), ((), ())), preferred_element_type=jnp.float32
    )


def multiply_left_transposed(left, right):
    return lax.dot_general(
        left, right, (((0,), (0,)), ((), ())), preferred_element_type=jnp.float32
    )


def pointwise(gate_activation, up_activation, backward_result):
    sigmoid_gate = jax.nn.sigmoid(gate_activation)
    silu_gate = gate_activation * sigmoid_gate
    hidden_state = (silu_gate * up_activation).astype(jnp.bfloat16)
    up_gradient_term = (backward_result * silu_gate).astype(jnp.bfloat16)
    gate_gradient_term = (
        backward_result
        * up_activation
        * sigmoid_gate
        * (1.0 + gate_activation * (1.0 - sigmoid_gate))
    ).astype(jnp.bfloat16)
    return (hidden_state, gate_gradient_term, up_gradient_term)


def shifted(size, step):
    return [(i, (i + step) % size) for i in range(size)]


def ring_sums(block_ofs, axis, ways):
    size = lax.axis_size(axis)
    here = lax.axis_index(axis)
    far = size // 2

    def block(stream, offset):
        return block_ofs[stream](lax.rem(here + offset * ways[stream] + size, size))

    def send(stream, value, step):
        return lax.ppermute(
            value.astype(jnp.bfloat16), axis, shifted(size, step * ways[stream])
        ).astype(jnp.float32)

    streams = range(len(ways))
    ahead = []
    behind = []
    for stream in streams:
        ahead.append(
            send(stream, block(stream, far), 2) + send(stream, block(stream, far - 1), 1)
        )
        behind.append(send(stream, block(stream, 1 - far), -1))
    for offset in range(far - 2, 0, -1):
        for stream in streams:
            ahead[stream] = send(stream, ahead[stream] + block(stream, offset), 1)
            behind[stream] = send(stream, behind[stream] + block(stream, -offset), -1)
    return [ahead[stream] + behind[stream] + block(stream, 0) for stream in streams]


def gather_tokens(activations, output_gradient):
    tokens, width = activations.shape
    row_count = lax.axis_size("row")
    side = math.isqrt(row_count // 2)
    here = lax.axis_index("row")
    core = lax.rem(here, 2)
    x = here // (2 * side)
    y = lax.rem(here // 2, side)
    first_at = jnp.where(core == 0, x, y)
    second_at = jnp.where(core == 0, y, x)

    def moves(first, second):
        pairs = []
        for source in range(row_count):
            sx, sy, sc = source // (2 * side), source // 2 % side, source % 2
            step_x, step_y = (first, second) if sc == 0 else (second, first)
            pairs.append(
                (source, (((sx + step_x) % side) * side + (sy + step_y) % side) * 2 + sc)
            )
        return pairs

    swap = [(source, source ^ 1) for source in range(row_count)]

    def to_other_core(value):
        return lax.ppermute(value, "row", swap)

    mine = jnp.where(core == 0, activations, output_gradient)
    given = to_other_core(jnp.where(core == 0, output_gradient, activations))
    pair = jnp.concatenate(
        [jnp.where(core == 0, mine, given), jnp.where(core == 0, given, mine)], axis=0
    )
    slab = jnp.zeros((side,) + pair.shape, pair.dtype)
    slab = lax.dynamic_update_index_in_dim(slab, pair, first_at, 0)
    for step in (1, -1, 2):
        got = lax.ppermute(pair, "row", moves(step, 0))
        slab = lax.dynamic_update_index_in_dim(
            slab, got, lax.rem(first_at - step + side, side), 0
        )
    slab = slab.reshape(side * 2 * tokens, width)
    half = slab.shape[0] // 2

    before = lax.ppermute(slab, "row", moves(0, 1))
    after = lax.ppermute(slab, "row", moves(0, -1))
    far = jnp.concatenate(
        [
            lax.ppermute(slab[:half], "row", moves(0, 2)),
            lax.ppermute(slab[half:], "row", moves(0, -2)),
        ],
        axis=0,
    )
    gathered = jnp.zeros((2, side) + slab.shape, slab.dtype)
    for offset, part in ((0, slab), (-1, before), (1, after), (2, far)):
        for which, value, at in (
            (core, part, second_at),
            (1 - core, to_other_core(part), first_at),
        ):
            gathered = lax.dynamic_update_slice(
                gathered, value[None, None], (which, lax.rem(at + offset + side, side), 0, 0)
            )
    shape = (side, side, 2 * tokens, width)
    return gathered[0].reshape(shape), gathered[1].reshape(shape)


def body(
    activations,
    output_gradient,
    frozen_gate_weight,
    frozen_up_weight,
    frozen_down_weight,
    gate_adapter_first,
    gate_adapter_second,
    up_adapter_first,
    up_adapter_second,
    down_adapter_first,
    down_leave,
):
    share_tokens, width = activations.shape
    rank, hidden_units = gate_adapter_second.shape
    row_count = lax.axis_size("row")
    col_count = lax.axis_size("col")
    tokens_all = share_tokens * row_count
    col_tokens = tokens_all // col_count
    chips = row_count // 2
    core = lax.rem(lax.axis_index("row"), 2)
    cut = (hidden_units - rank) // 2
    wide_size = hidden_units - cut
    swap = [(i, i ^ 1) for i in range(row_count)]
    same_core = [[2 * chip + c for chip in range(chips)] for c in range(2)]

    gathered_act, gathered_out = gather_tokens(activations, output_gradient)
    side = gathered_act.shape[0]
    pair_tokens = 2 * share_tokens
    pairs_per_col = col_tokens // pair_tokens
    blocks_per_line = side // pairs_per_col
    full_act = gathered_act.reshape(tokens_all, width)
    full_out = gathered_out.reshape(tokens_all, width)

    def blocks_of(first, size):
        def lines_block(partial, index):
            lines = partial.reshape(side, side, pair_tokens, -1)
            place = (lax.rem(index, blocks_per_line) * pairs_per_col, index // blocks_per_line)
            chosen = lax.dynamic_slice(
                lines, place + (0, first), (pairs_per_col, 1, pair_tokens, size)
            )
            return chosen.reshape(col_tokens, size)

        def block_of(index):
            return jnp.stack(
                [
                    lines_block(partials[0], index),
                    lines_block(partials[1], index),
                    lax.dynamic_slice(
                        partials[2], (index * col_tokens, first), (col_tokens, size)
                    ),
                ]
            )

        return block_of

    def deltas_of(totals, low, columns):
        gate_activation = totals[0] + adapter_scale * matrix_multiply(
            low[0], gate_adapter_second[:, columns]
        )
        up_activation = totals[1] + adapter_scale * matrix_multiply(
            low[1], up_adapter_second[:, columns]
        )
        backward_result = totals[2] + adapter_scale * multiply_right_transposed(
            low[2], down_adapter_first[columns]
        )
        return pointwise(gate_activation, up_activation, backward_result)

    partials = lax.optimization_barrier(
        (
            multiply_right_transposed(
                full_act, jnp.concatenate([frozen_gate_weight, gate_adapter_first], axis=1).T
            ),
            multiply_right_transposed(
                full_act, jnp.concatenate([frozen_up_weight, up_adapter_first], axis=1).T
            ),
            multiply_right_transposed(
                full_out, jnp.concatenate([frozen_down_weight, down_leave], axis=0)
            ),
        )
    )
    later = slice(cut, hidden_units)
    earlier = slice(0, cut)
    totals, second_totals = ring_sums(
        (blocks_of(cut, wide_size + rank), blocks_of(0, cut)), "col", (1, -1)
    )
    low = totals[:, :, wide_size:].astype(jnp.bfloat16)
    later_deltas = deltas_of(totals[:, :, :wide_size], low, later)
    earlier_deltas = deltas_of(second_totals, low, earlier)

    packed = jnp.concatenate(
        [
            piece
            for which, rank_part in ((1, low[0]), (2, low[1]), (0, low[2]))
            for piece in (earlier_deltas[which], later_deltas[which], rank_part)
        ],
        axis=1,
    )
    piece = lax.all_gather(packed, "col", axis=0, tiled=True)
    packed_width = hidden_units + rank

    def packed_part(which):
        return packed[:, which * packed_width : which * packed_width + hidden_units]

    own_factors = jnp.concatenate(
        [
            matrix_multiply(packed_part(2), down_adapter_first),
            multiply_right_transposed(packed_part(0), gate_adapter_second),
            multiply_right_transposed(packed_part(1), up_adapter_second),
        ],
        axis=1,
    ).astype(jnp.bfloat16)

    def to_all(value, axis, count, groups=None):
        copies = jnp.broadcast_to(value[None], (count,) + value.shape)
        return lax.all_to_all(copies, axis, 0, 0, axis_index_groups=groups, tiled=True)

    other_factors = lax.ppermute(own_factors, "row", swap)
    own_factors = own_factors.astype(jnp.float32) + other_factors.astype(jnp.float32)
    factor_parts = to_all(own_factors.astype(jnp.bfloat16), "row", chips, same_core)
    own_factors = jnp.sum(factor_parts.astype(jnp.float32), axis=0).astype(jnp.bfloat16)
    factors = to_all(own_factors, "col", col_count).reshape(tokens_all, 3 * rank)
    piece, factors = lax.optimization_barrier((piece, factors))
    piece_gate, piece_up = [
        piece[:, i * packed_width : i * packed_width + hidden_units] for i in range(2)
    ]

    def input_part(which):
        def term(deltas, weight):
            lines = deltas.reshape(chips, 2, share_tokens, hidden_units)
            chosen = lax.dynamic_index_in_dim(lines, which, 1, keepdims=False)
            return multiply_right_transposed(
                chosen.reshape(chips * share_tokens, hidden_units), weight
            )

        return term(piece_gate, frozen_gate_weight) + term(piece_up, frozen_up_weight)

    other = lax.ppermute(input_part(1 - core).astype(jnp.bfloat16), "row", swap)
    share = (input_part(core) + other.astype(jnp.float32)).astype(jnp.bfloat16)
    factors, piece, share = lax.optimization_barrier((factors, piece, share))
    shares = lax.all_to_all(share, "row", 0, 0, axis_index_groups=same_core, tiled=True)
    summed = jnp.sum(shares.reshape(chips, share_tokens, width).astype(jnp.float32), axis=0)

    first_token = lax.axis_index("row") * share_tokens
    row_factors = lax.dynamic_slice_in_dim(factors, first_token, share_tokens, 0)
    activation_gradient = (
        summed
        + adapter_scale
        * (
            multiply_right_transposed(row_factors[:, rank : 2 * rank], gate_adapter_first)
            + multiply_right_transposed(row_factors[:, 2 * rank :], up_adapter_first)
        )
    ).astype(jnp.bfloat16)

    features = width // row_count
    first_feature = lax.axis_index("row") * features
    activation_columns = lax.dynamic_slice_in_dim(full_act, first_feature, features, 1)
    activation_columns = activation_columns.reshape(side, side, pair_tokens, features)
    activation_columns = activation_columns.swapaxes(0, 1).reshape(tokens_all, features)
    output_columns = lax.dynamic_slice_in_dim(full_out, first_feature, features, 1)
    first_gradients = adapter_scale * multiply_left_transposed(
        activation_columns, factors[:, rank:]
    )
    gate_adapter_first_gradient = first_gradients[:, :rank]
    up_adapter_first_gradient = first_gradients[:, rank:]
    down_adapter_second_gradient = adapter_scale * multiply_left_transposed(
        factors[:, :rank], output_columns
    )

    piece_gate, piece_up, piece_hidden = [
        piece[:, i * packed_width : i * packed_width + hidden_units] for i in range(3)
    ]
    gate_low, up_low, down_low = [
        piece[:, i * packed_width + hidden_units : (i + 1) * packed_width] for i in range(3)
    ]
    gate_adapter_second_gradient = adapter_scale * multiply_left_transposed(gate_low, piece_gate)
    up_adapter_second_gradient = adapter_scale * multiply_left_transposed(up_low, piece_up)
    down_adapter_first_gradient = adapter_scale * multiply_left_transposed(piece_hidden, down_low)
    return (
        activation_gradient,
        gate_adapter_first_gradient,
        gate_adapter_second_gradient,
        up_adapter_first_gradient,
        up_adapter_second_gradient,
        down_adapter_first_gradient,
        down_adapter_second_gradient,
    )


def solution(mesh):
    return jax.shard_map(
        body,
        mesh=mesh,
        in_specs=(
            P("row", "col"),
            P("row", "col"),
            P("col", "row"),
            P("col", "row"),
            P("row", "col"),
            P("col", None),
            P(None, "row"),
            P("col", None),
            P(None, "row"),
            P("row", None),
            P(None, "col"),
        ),
        out_specs=(
            P("row", "col"),
            P(("col", "row"), None),
            P(None, "row"),
            P(("col", "row"), None),
            P(None, "row"),
            P("row", None),
            P(None, ("col", "row")),
        ),
        check_vma=False,
    )
```

```python
import math

import jax
import jax.numpy as jnp
from jax import lax
from jax.sharding import PartitionSpec as P

adapter_scale = 0.5


def matrix_multiply(left, right):
    return jnp.dot(left, right, preferred_element_type=jnp.float32)


def multiply_right_transposed(left, right):
    return lax.dot_general(
        left, right, (((1,), (1,)), ((), ())), preferred_element_type=jnp.float32
    )


def multiply_left_transposed(left, right):
    return lax.dot_general(
        left, right, (((0,), (0,)), ((), ())), preferred_element_type=jnp.float32
    )


def pointwise(gate_activation, up_activation, backward_result):
    sigmoid_gate = jax.nn.sigmoid(gate_activation)
    silu_gate = gate_activation * sigmoid_gate
    hidden_state = (silu_gate * up_activation).astype(jnp.bfloat16)
    up_gradient_term = (backward_result * silu_gate).astype(jnp.bfloat16)
    gate_gradient_term = (
        backward_result
        * up_activation
        * sigmoid_gate
        * (1.0 + gate_activation * (1.0 - sigmoid_gate))
    ).astype(jnp.bfloat16)
    return (hidden_state, gate_gradient_term, up_gradient_term)


def shifted(size, step):
    return [(i, (i + step) % size) for i in range(size)]


def ring_sums(block_ofs, axis, ways):
    size = lax.axis_size(axis)
    here = lax.axis_index(axis)
    far = size // 2

    def block(stream, offset):
        return block_ofs[stream](lax.rem(here + offset * ways[stream] + size, size))

    def send(stream, value, step):
        return lax.ppermute(
            value.astype(jnp.bfloat16), axis, shifted(size, step * ways[stream])
        ).astype(jnp.float32)

    streams = range(len(ways))
    ahead = []
    behind = []
    for stream in streams:
        ahead.append(
            send(stream, block(stream, far), 2) + send(stream, block(stream, far - 1), 1)
        )
        behind.append(send(stream, block(stream, 1 - far), -1))
    for offset in range(far - 2, 0, -1):
        for stream in streams:
            ahead[stream] = send(stream, ahead[stream] + block(stream, offset), 1)
            behind[stream] = send(stream, behind[stream] + block(stream, -offset), -1)
    return [ahead[stream] + behind[stream] + block(stream, 0) for stream in streams]


def gather_tokens(activations, output_gradient):
    tokens, width = activations.shape
    row_count = lax.axis_size("row")
    side = math.isqrt(row_count // 2)
    here = lax.axis_index("row")
    core = lax.rem(here, 2)
    x = here // (2 * side)
    y = lax.rem(here // 2, side)
    first_at = jnp.where(core == 0, x, y)
    second_at = jnp.where(core == 0, y, x)

    def moves(first, second):
        pairs = []
        for source in range(row_count):
            sx, sy, sc = source // (2 * side), source // 2 % side, source % 2
            step_x, step_y = (first, second) if sc == 0 else (second, first)
            pairs.append(
                (source, (((sx + step_x) % side) * side + (sy + step_y) % side) * 2 + sc)
            )
        return pairs

    swap = [(source, source ^ 1) for source in range(row_count)]

    def to_other_core(value):
        return lax.ppermute(value, "row", swap)

    mine = jnp.where(core == 0, activations, output_gradient)
    given = to_other_core(jnp.where(core == 0, output_gradient, activations))
    pair = jnp.concatenate(
        [jnp.where(core == 0, mine, given), jnp.where(core == 0, given, mine)], axis=0
    )
    slab = jnp.zeros((side,) + pair.shape, pair.dtype)
    slab = lax.dynamic_update_index_in_dim(slab, pair, first_at, 0)
    for step in (1, -1, 2):
        got = lax.ppermute(pair, "row", moves(step, 0))
        slab = lax.dynamic_update_index_in_dim(
            slab, got, lax.rem(first_at - step + side, side), 0
        )
    slab = slab.reshape(side * 2 * tokens, width)
    half = slab.shape[0] // 2

    before = lax.ppermute(slab, "row", moves(0, 1))
    after = lax.ppermute(slab, "row", moves(0, -1))
    far = jnp.concatenate(
        [
            lax.ppermute(slab[:half], "row", moves(0, 2)),
            lax.ppermute(slab[half:], "row", moves(0, -2)),
        ],
        axis=0,
    )
    gathered = jnp.zeros((2, side) + slab.shape, slab.dtype)
    for offset, part in ((0, slab), (-1, before), (1, after), (2, far)):
        for which, value, at in (
            (core, part, second_at),
            (1 - core, to_other_core(part), first_at),
        ):
            gathered = lax.dynamic_update_slice(
                gathered, value[None, None], (which, lax.rem(at + offset + side, side), 0, 0)
            )
    shape = (side, side, 2 * tokens, width)
    return gathered[0].reshape(shape), gathered[1].reshape(shape)


def body(
    activations,
    output_gradient,
    frozen_gate_weight,
    frozen_up_weight,
    frozen_down_weight,
    gate_adapter_first,
    gate_adapter_second,
    up_adapter_first,
    up_adapter_second,
    down_adapter_first,
    down_leave,
):
    share_tokens, width = activations.shape
    rank, hidden_units = gate_adapter_second.shape
    row_count = lax.axis_size("row")
    col_count = lax.axis_size("col")
    tokens_all = share_tokens * row_count
    col_tokens = tokens_all // col_count
    chips = row_count // 2
    core = lax.rem(lax.axis_index("row"), 2)
    cut = (hidden_units - rank) // 2
    wide_size = hidden_units - cut
    swap = [(i, i ^ 1) for i in range(row_count)]
    same_core = [[2 * chip + c for chip in range(chips)] for c in range(2)]

    gathered_act, gathered_out = gather_tokens(activations, output_gradient)
    side = gathered_act.shape[0]
    pair_tokens = 2 * share_tokens
    pairs_per_col = col_tokens // pair_tokens
    blocks_per_line = side // pairs_per_col
    full_act = gathered_act.reshape(tokens_all, width)
    full_out = gathered_out.reshape(tokens_all, width)

    def blocks_of(first, size):
        def lines_block(partial, index):
            lines = partial.reshape(side, side, pair_tokens, -1)
            place = (lax.rem(index, blocks_per_line) * pairs_per_col, index // blocks_per_line)
            chosen = lax.dynamic_slice(
                lines, place + (0, first), (pairs_per_col, 1, pair_tokens, size)
            )
            return chosen.reshape(col_tokens, size)

        def block_of(index):
            return jnp.stack(
                [
                    lines_block(partials[0], index),
                    lines_block(partials[1], index),
                    lax.dynamic_slice(
                        partials[2], (index * col_tokens, first), (col_tokens, size)
                    ),
                ]
            )

        return block_of

    def deltas_of(totals, low, columns):
        gate_activation = totals[0] + adapter_scale * matrix_multiply(
            low[0], gate_adapter_second[:, columns]
        )
        up_activation = totals[1] + adapter_scale * matrix_multiply(
            low[1], up_adapter_second[:, columns]
        )
        backward_result = totals[2] + adapter_scale * multiply_right_transposed(
            low[2], down_adapter_first[columns]
        )
        return pointwise(gate_activation, up_activation, backward_result)

    partials = lax.optimization_barrier(
        (
            multiply_right_transposed(
                full_act, jnp.concatenate([frozen_gate_weight, gate_adapter_first], axis=1).T
            ),
            multiply_right_transposed(
                full_act, jnp.concatenate([frozen_up_weight, up_adapter_first], axis=1).T
            ),
            multiply_right_transposed(
                full_out, jnp.concatenate([frozen_down_weight, down_leave], axis=0)
            ),
        )
    )
    later = slice(cut, hidden_units)
    earlier = slice(0, cut)
    totals, second_totals = ring_sums(
        (blocks_of(cut, wide_size + rank), blocks_of(0, cut)), "col", (1, -1)
    )
    low = totals[:, :, wide_size:].astype(jnp.bfloat16)
    later_deltas = deltas_of(totals[:, :, :wide_size], low, later)
    earlier_deltas = deltas_of(second_totals, low, earlier)

    packed = jnp.concatenate(
        [
            piece
            for which, rank_part in ((1, low[0]), (2, low[1]), (0, low[2]))
            for piece in (earlier_deltas[which], later_deltas[which], rank_part)
        ],
        axis=1,
    )
    piece = lax.all_gather(packed, "col", axis=0, tiled=True)
    packed_width = hidden_units + rank

    def packed_part(which):
        return packed[:, which * packed_width : which * packed_width + hidden_units]

    own_factors = jnp.concatenate(
        [
            matrix_multiply(packed_part(2), down_adapter_first),
            multiply_right_transposed(packed_part(0), gate_adapter_second),
            multiply_right_transposed(packed_part(1), up_adapter_second),
        ],
        axis=1,
    ).astype(jnp.bfloat16)

    def to_all(value, axis, count, groups=None):
        copies = jnp.broadcast_to(value[None], (count,) + value.shape)
        return lax.all_to_all(copies, axis, 0, 0, axis_index_groups=groups, tiled=True)

    other_factors = lax.ppermute(own_factors, "row", swap)
    own_factors = own_factors.astype(jnp.float32) + other_factors.astype(jnp.float32)
    half_tokens = col_tokens // 2
    own_factors = jnp.concatenate(
        [
            own_factors[:, : 2 * rank],
            jnp.concatenate(
                [own_factors[:half_tokens, 2 * rank :], own_factors[half_tokens:, 2 * rank :]],
                axis=1,
            ),
        ],
        axis=0,
    )
    factor_parts = to_all(own_factors.astype(jnp.bfloat16), "row", chips, same_core)
    own_factors = jnp.sum(factor_parts.astype(jnp.float32), axis=0).astype(jnp.bfloat16)
    factors = to_all(own_factors, "col", col_count)
    last = factors[:, col_tokens:]
    last = jnp.concatenate([last[:, :, :rank], last[:, :, rank:]], axis=1)
    factors = jnp.concatenate([factors[:, :col_tokens], last], axis=2)
    factors = factors.reshape(tokens_all, 3 * rank)
    piece, factors = lax.optimization_barrier((piece, factors))
    piece_gate, piece_up, piece_hidden = [
        piece[:, i * packed_width : i * packed_width + hidden_units] for i in range(3)
    ]
    gate_low, up_low, down_low = [
        piece[:, i * packed_width + hidden_units : (i + 1) * packed_width] for i in range(3)
    ]

    def input_part(which):
        def term(deltas, weight):
            lines = deltas.reshape(chips, 2, share_tokens, hidden_units)
            chosen = lax.dynamic_index_in_dim(lines, which, 1, keepdims=False)
            return multiply_right_transposed(
                chosen.reshape(chips * share_tokens, hidden_units), weight
            )

        return term(piece_gate, frozen_gate_weight) + term(piece_up, frozen_up_weight)

    other = lax.ppermute(input_part(1 - core).astype(jnp.bfloat16), "row", swap)
    share = (input_part(core) + other.astype(jnp.float32)).astype(jnp.bfloat16)
    shares = lax.all_to_all(share, "row", 0, 0, axis_index_groups=same_core, tiled=True)
    summed = jnp.sum(shares.reshape(chips, share_tokens, width).astype(jnp.float32), axis=0)

    first_token = lax.axis_index("row") * share_tokens
    row_factors = lax.dynamic_slice_in_dim(factors, first_token, share_tokens, 0)
    activation_gradient = (
        summed
        + adapter_scale
        * (
            multiply_right_transposed(row_factors[:, rank : 2 * rank], gate_adapter_first)
            + multiply_right_transposed(row_factors[:, 2 * rank :], up_adapter_first)
        )
    ).astype(jnp.bfloat16)

    features = width // row_count
    first_feature = lax.axis_index("row") * features
    activation_columns = lax.dynamic_slice_in_dim(full_act, first_feature, features, 1)
    activation_columns = activation_columns.reshape(side, side, pair_tokens, features)
    activation_columns = activation_columns.swapaxes(0, 1).reshape(tokens_all, features)
    output_columns = lax.dynamic_slice_in_dim(full_out, first_feature, features, 1)
    first_gradients = adapter_scale * multiply_left_transposed(
        activation_columns, factors[:, rank:]
    )
    gate_adapter_first_gradient = first_gradients[:, :rank]
    up_adapter_first_gradient = first_gradients[:, rank:]
    down_adapter_second_gradient = adapter_scale * multiply_left_transposed(
        factors[:, :rank], output_columns
    )

    gate_adapter_second_gradient = adapter_scale * multiply_left_transposed(gate_low, piece_gate)
    up_adapter_second_gradient = adapter_scale * multiply_left_transposed(up_low, piece_up)
    down_adapter_first_gradient = adapter_scale * multiply_left_transposed(piece_hidden, down_low)
    return (
        activation_gradient,
        gate_adapter_first_gradient,
        gate_adapter_second_gradient,
        up_adapter_first_gradient,
        up_adapter_second_gradient,
        down_adapter_first_gradient,
        down_adapter_second_gradient,
    )


def solution(mesh):
    return jax.shard_map(
        body,
        mesh=mesh,
        in_specs=(
            P("row", "col"),
            P("row", "col"),
            P("col", "row"),
            P("col", "row"),
            P("row", "col"),
            P("col", None),
            P(None, "row"),
            P("col", None),
            P(None, "row"),
            P("row", None),
            P(None, "col"),
        ),
        out_specs=(
            P("row", "col"),
            P(("col", "row"), None),
            P(None, "row"),
            P(("col", "row"), None),
            P(None, "row"),
            P("row", None),
            P(None, ("col", "row")),
        ),
        check_vma=False,
    )
```
